256 devices in a mesh: dp: 4 (over y), seq: 64 (over z, x, core).
Axes of the slice: x: 4, y: 4, z: 8, core: 2. Of those that a mesh axis runs over, the one named last changes fastest.
Arguments:
- qkv: bfloat16 [4, 12, 16384, 384], P('dp', None, 'seq'), may hold values from -12 to 12
- out_weight: bfloat16 [1536, 1536], P(('dp', 'seq')), may hold values from -0.5 to 0.5
- grad_projected: bfloat16 [4, 16384, 1536], P('dp', 'seq'), may hold values from -1.5 to 1.5
- group_span: int32 [4, 64], P('dp'), may hold values from 1 to 4, as said below
- clip_length: int32 [4, 64], P('dp'), may hold values from 16 to 1024, as said below
Outputs:
- projected: bfloat16 [4, 16384, 1536], P('dp', 'seq')
- grad_qkv: bfloat16 [4, 12, 16384, 384], P('dp', None, 'seq')
- grad_weight: float32 [1536, 1536], P(('dp', 'seq'))
The draws below stay inside these ranges and needn't reach their ends.
Inputs may be any that keep to these rules, and one draw needn't show every extreme that they name: `group_span`: each entry is a power of two; along seq the devices of each row form aligned groups of that many consecutive devices, every device holding its group's size; the first 4 devices of every row form one group. `clip_length`: equal on all devices of a group; for a group of g devices it lies between (g - 1) * 256 + 16 and g * 256; the group of the first 4 devices of every row has length 1024.
All inputs are finite; a program needn't handle non-finite values.
Results may differ from the reference program's by a relative error of at most 0.012.
The reference program's roundings to bfloat16 on the way count: a program that leaves them out, or rounds other values in their place, can miss the bound.
Values may be sent and summed in bfloat16 or wider, within the bound.
A program may use at most 128 MiB of HBM per device.

```python
import jax
import jax.numpy as jnp
from jax import lax

HEADS = 12
HEAD_DIM = 128
WIDTH = 1536
TOK = 256
SECTIONS = 2
GROUP_MAX = 4
TOKENS = 16384
N_DP = 4
N_SEQ = 64


def group_sizes(key):
    spans_now = jnp.full((N_DP, N_SEQ), GROUP_MAX, jnp.int32)
    device = jnp.arange(N_SEQ, dtype=jnp.int32)
    for depth_index in range(SECTIONS):
        width_now = GROUP_MAX >> depth_index
        coin_flips = jax.random.randint(jax.random.fold_in(key, 100 + depth_index), (N_DP, N_SEQ // width_now), 0, 2)
        coin_flips = jnp.repeat(coin_flips, width_now, axis=1)
        coin_flips = jnp.where(device[None, :] < GROUP_MAX, 0, coin_flips)
        spans_now = jnp.where((spans_now == width_now) & (coin_flips == 1), width_now // 2, spans_now)
    return spans_now


def draw_group_span(key, part):
    return group_sizes(key)


def draw_clip_length(key, part):
    spans_now = group_sizes(key)
    key = jax.random.fold_in(key, 7)
    lowest = max(TOK // 16, 3)
    fills = jax.random.randint(key, (N_DP, N_SEQ), lowest, TOK + 1)
    device = jnp.arange(N_SEQ, dtype=jnp.int32)[None, :]
    fills = jnp.where(device < GROUP_MAX, TOK, fills)
    starts = device - device % spans_now
    start_fill = jnp.take_along_axis(fills, starts, axis=1)
    return (spans_now - 1) * TOK + start_fill


def draw_qkv(key, part):
    key = jax.random.fold_in(key, 11)
    shape_full = (N_DP, HEADS, TOKENS, 3 * HEAD_DIM)
    values = jnp.clip(jax.random.normal(key, shape_full, jnp.float32), -6.0, 6.0)
    return values.astype(jnp.bfloat16)


def level_of(key, extent, cuts, least, high):
    factor_of = 1.0
    for axis_at, shards_of in cuts:
        heights = jax.random.uniform(jax.random.fold_in(jax.random.fold_in(key, 6), axis_at), (shards_of,), jnp.float32, least / len(cuts), high / len(cuts))
        factor_of = factor_of * jnp.repeat(jnp.exp(heights), extent[axis_at] // shards_of).reshape((-1,) + (1,) * (len(extent) - 1 - axis_at))
    return factor_of


def scatter_about(key, shape, spread, most, pieces=(), kind=jnp.bfloat16):
    drawn = spread * jax.random.normal(key, shape, jnp.float32)
    if pieces:
        drawn = drawn * level_of(key, shape, pieces, -0.22, 0.18)
    return jnp.clip(drawn, -most, most).astype(kind)


def setup_inputs(seed: int = 0) -> dict:
    splits = jax.random.split(jax.random.key(seed), 6)
    return {
        "qkv": draw_qkv(jax.random.fold_in(splits[5], 71), 0),
        "out_weight": scatter_about(splits[1], (HEADS * HEAD_DIM, WIDTH), HEAD_DIM ** -0.5, 0.5, ((0, 256),)),
        "grad_projected": scatter_about(splits[2], (N_DP, TOKENS, WIDTH), 0.25, 1.5, ((0, 4), (1, 64))),
        "group_span": draw_group_span(jax.random.fold_in(splits[5], 71), 0),
        "clip_length": draw_clip_length(jax.random.fold_in(splits[5], 71), 0),
    }


SCORE_FLOOR = -1.0e30


def settle(values):
    return lax.optimization_barrier(values.astype(jnp.bfloat16))


def block_mask(spans, lengths):
    token_index = jnp.arange(GROUP_MAX * TOK, dtype=jnp.int32)
    device = token_index // TOK
    own_span = spans[device]
    start_device = device - device % own_span
    position = (device - start_device) * TOK + token_index % TOK
    key_live = position < lengths[device]
    return (start_device[:, None] == start_device[None, :]) & key_live[None, :]


def block_attention(block):
    packed, grad_heads, spans, lengths = block
    allowed = block_mask(spans, lengths)
    queries = packed[..., :HEAD_DIM].astype(jnp.float32)
    keys_all = packed[..., HEAD_DIM:2 * HEAD_DIM].astype(jnp.float32)
    values_all = packed[..., 2 * HEAD_DIM:].astype(jnp.float32)
    score_scale = HEAD_DIM ** -0.5
    scores = jnp.einsum("hqd,hkd->hqk", queries, keys_all) * score_scale
    scores = jnp.where(allowed, scores, SCORE_FLOOR)
    top_score = jnp.max(scores, axis=-1, keepdims=True)
    totals = jnp.sum(jnp.where(allowed, jnp.exp(scores - top_score), 0.0), axis=-1, keepdims=True)
    log_total = top_score + jnp.log(totals)
    probabilities = jnp.where(allowed, jnp.exp(scores - log_total), 0.0)
    prob_half = settle(probabilities).astype(jnp.float32)
    attended = settle(jnp.einsum("hqk,hkd->hqd", prob_half, values_all))
    grad_wide = grad_heads.astype(jnp.float32)
    row_delta = jnp.sum(grad_wide * attended.astype(jnp.float32), axis=-1, keepdims=True)
    grad_probs = jnp.einsum("hqd,hkd->hqk", grad_wide, values_all)
    grad_scores = settle(probabilities * (grad_probs - row_delta)).astype(jnp.float32)
    query_grad = jnp.einsum("hqk,hkd->hqd", grad_scores, keys_all) * score_scale
    key_grad = jnp.einsum("hqk,hqd->hkd", grad_scores, queries) * score_scale
    value_grad = jnp.einsum("hqk,hqd->hkd", prob_half, grad_wide)
    grad_packed = jnp.concatenate([query_grad, key_grad, value_grad], axis=-1).astype(jnp.bfloat16)
    return attended, grad_packed


def reference(qkv, out_weight, grad_projected, group_span, clip_length):
    blocks_per_row = N_SEQ // GROUP_MAX
    block_tokens = GROUP_MAX * TOK
    width_heads = HEADS * HEAD_DIM
    grad_flat = grad_projected.reshape(N_DP * TOKENS, WIDTH)
    grad_attended = jnp.dot(grad_flat, out_weight.T, preferred_element_type=jnp.float32).astype(jnp.bfloat16)
    grad_attended = grad_attended.reshape(N_DP, TOKENS, HEADS, HEAD_DIM).transpose(0, 2, 1, 3)

    def to_blocks(array):
        last_dim = array.shape[-1]
        shaped = array.reshape(N_DP, HEADS, blocks_per_row, block_tokens, last_dim)
        return shaped.transpose(0, 2, 1, 3, 4).reshape(N_DP * blocks_per_row, HEADS, block_tokens, last_dim)

    def from_blocks(array):
        last_dim = array.shape[-1]
        shaped = array.reshape(N_DP, blocks_per_row, HEADS, block_tokens, last_dim)
        return shaped.transpose(0, 2, 1, 3, 4).reshape(N_DP, HEADS, TOKENS, last_dim)

    spans_blocks = group_span.reshape(N_DP * blocks_per_row, GROUP_MAX)
    lengths_blocks = clip_length.reshape(N_DP * blocks_per_row, GROUP_MAX)
    attended, grad_packed = lax.map(block_attention, (to_blocks(qkv), to_blocks(grad_attended), spans_blocks, lengths_blocks))
    attended = from_blocks(attended)
    grad_qkv = from_blocks(grad_packed)
    attended_rows = attended.transpose(0, 2, 1, 3).reshape(N_DP * TOKENS, width_heads)
    projected = jnp.dot(attended_rows, out_weight, preferred_element_type=jnp.float32).astype(jnp.bfloat16)
    projected = projected.reshape(N_DP, TOKENS, WIDTH)
    grad_weight = jnp.dot(attended_rows.T, grad_flat, preferred_element_type=jnp.float32)
    return projected, grad_qkv, grad_weight
```

```python
import functools

import jax
import jax.numpy as jnp
from jax import lax
from jax.experimental import pallas as pl
from jax.experimental.pallas import tpu as pltpu
from jax.sharding import PartitionSpec as P

HEADS = 12
DIM = 128
TOK = 256
WIDTH = 1536
HALF = WIDTH // 2
NY = 4
NZ = 8
NX = 4
SLAB = 48
BLOCK = SLAB * NZ
OWN_HEADS = HEADS // NY
CHIP_ROWS = 12
DEV_ROWS = 6
AHEAD = 4
FLOOR = -1e30
SCALE = DIM**-0.5
LOG2E = 1.4426950408889634
MESH = pl.DeviceIdType.MESH
F32 = jnp.float32
BF16 = jnp.bfloat16


def mm(a, b, dims):
    return lax.dot_general(a, b, (dims, ((), ())), preferred_element_type=F32)


NN = ((1,), (0,))
NT = ((1,), (1,))
TN = ((0,), (0,))


def kernel(
    qkv, w_own, gp, span, clip,
    proj_o, grad_o, gw_o,
    q_s, kv, bias_s, w_all, o_s, lse_s,
    w_send, w_pair, w_tmp, w_x, w_slab,
    g_tmp, g_acc, g_send, g_recv, gy_send, gy_recv, gz_send, gz_recv,
    gx_in, gx_send, gx_recv, gc_send, gc_recv,
    d_own, d_rs, d_sib, d_sib_r, d_x, d_x_r,
    loc_sem, ks_s, ks_r, kx_s, kx_r, kf_s, kf_r,
    wa_s, wa_r, wx_s, wx_r, wz_s, wz_r, wy_s, wy_r, wf_s, wf_r, wb_s, wb_r,
    gs_s, gs_r, gy_s, gy_r, gz_s, gz_r, gx_s, gx_r, gc_s, gc_r,
    ds_s, ds_r, dx_s, dx_r,
):
    me = lax.axis_index("seq")
    y = lax.axis_index("dp")
    c = me % 2
    x = (me // 2) % NX
    z = me // (2 * NX)
    sib = me + 1 - 2 * c
    far = me + 2 - 4 * (x % 2)
    cross = far + 1 - 2 * c

    def at_x(xx):
        return {"seq": (z * NX + xx) * 2 + c}

    def at_z(zz):
        return {"seq": (zz * NX + x) * 2 + c}

    def at_y(yy):
        return {"dp": yy}

    at_sib = {"seq": sib}
    at_far = {"seq": far}

    def rdma(src, dst, send, recv, device):
        return pltpu.make_async_remote_copy(
            src_ref=src, dst_ref=dst, send_sem=send, recv_sem=recv,
            device_id=device, device_id_type=MESH,
        )

    partners = [at_sib]
    partners += [at_x((x + d) % NX) for d in range(1, NX)]
    partners += [at_z((z + d) % NZ) for d in range(1, NZ)]
    partners += [at_y((y + d) % NY) for d in range(1, NY)]
    barrier = pltpu.get_barrier_semaphore()
    for partner in partners:
        pl.semaphore_signal(barrier, inc=1, device_id=partner, device_id_type=MESH)
    pl.semaphore_wait(barrier, len(partners))

    def head(i):
        return (OWN_HEADS * (y + 1) + i) % HEADS

    def kv_sib(i):
        return rdma(qkv.at[0, head(i), :, pl.ds(DIM, 2 * DIM)], kv.at[i, 1], ks_s.at[i], ks_r.at[i], at_sib)

    def kv_far(i):
        return rdma(qkv.at[0, head(i), :, pl.ds(DIM, 2 * DIM)], kv.at[i, 2], kx_s.at[i], kx_r.at[i], at_far)

    def kv_relay(i):
        return rdma(kv.at[i, 2], kv.at[i, 3], kf_s.at[i], kf_r.at[i], at_sib)

    def kv_own(i):
        return pltpu.make_async_copy(qkv.at[0, head(i), :, pl.ds(DIM, 2 * DIM)], kv.at[i, 0], loc_sem.at[1 + i])

    q_copy = pltpu.make_async_copy(qkv.at[0, :, :, pl.ds(0, DIM)], q_s, loc_sem.at[0])

    mine = pl.ds(pl.multiple_of(c * HALF, HALF), HALF)
    other = pl.ds(pl.multiple_of((1 - c) * HALF, HALF), HALF)

    def slab(yy, zz):
        return w_all.at[pl.ds(pl.multiple_of(SLAB * (NZ * yy + zz), 16), SLAB), mine]

    pair_copy = rdma(w_send, w_pair.at[c], wa_s, wa_r, at_sib)
    pair_wait = rdma(w_send, w_pair.at[1 - c], wa_s, wa_r, at_sib)

    def x_copy(d):
        return rdma(w_x.at[x], w_x.at[x], wx_s.at[d - 1], wx_r.at[d - 1], at_x((x + d) % NX))

    def x_wait(d):
        back = (x + NX - d) % NX
        return rdma(w_x.at[back], w_x.at[back], wx_s.at[d - 1], wx_r.at[d - 1], at_x(back))

    def z_copy(d):
        return rdma(slab(y, z), slab(y, z), wz_s.at[d - 1], wz_r.at[d - 1], at_z((z + d) % NZ))

    def z_wait(d):
        back = (z + NZ - d) % NZ
        return rdma(slab(y, back), slab(y, back), wz_s.at[d - 1], wz_r.at[d - 1], at_z(back))

    up, down = (y + 1) % NY, (y + NY - 1) % NY
    opposite = (y + 2) % NY

    def y_copy(d, way):
        zz = (z + NZ - d) % NZ
        return rdma(slab(y, zz), slab(y, zz), wy_s.at[d, way], wy_r.at[d, way], at_y(up if way == 0 else down))

    def y_wait(d, way):
        zz = (z + NZ - d) % NZ
        yy = down if way == 0 else up
        return rdma(slab(yy, zz), slab(yy, zz), wy_s.at[d, way], wy_r.at[d, way], at_y(yy))

    def y_relay(d):
        zz = (z + NZ - d) % NZ
        odd = d % 2
        yy = (y + NY - 1 + 2 * odd) % NY
        to = (y + 1 + 2 * odd) % NY
        return rdma(slab(yy, zz), slab(yy, zz), wf_s.at[d], wf_r.at[d], at_y(to))

    def y_relay_wait(d):
        zz = (z + NZ - d) % NZ
        return rdma(slab(opposite, zz), slab(opposite, zz), wf_s.at[d], wf_r.at[d], at_y(up))

    def rows_block(yy, columns):
        return w_all.at[pl.ds(pl.multiple_of(BLOCK * yy, 16), BLOCK), columns]

    def block_copy(k):
        yy = (y, down, up, opposite)[k]
        return rdma(rows_block(yy, mine), rows_block(yy, mine), wb_s.at[k], wb_r.at[k], at_sib)

    def block_wait(k):
        yy = (y, down, up, opposite)[k]
        return rdma(rows_block(yy, other), rows_block(yy, other), wb_s.at[k], wb_r.at[k], at_sib)

    def z_order(i):
        return 1 + i // 2 + (i % 2) * (NZ - 2 - 2 * (i // 2))

    def g_pair(i):
        return rdma(g_send.at[i], g_recv.at[i], gs_s.at[i], gs_r.at[i], at_sib)

    def g_y(i):
        return rdma(gy_send.at[i], gy_recv.at[i], gy_s.at[i], gy_r.at[i], at_y((y + 1 + i // OWN_HEADS) % NY))

    def g_z(d):
        zz = (z + d) % NZ
        rows = gz_send.at[pl.ds(pl.multiple_of(SLAB * zz, 16), SLAB)]
        return rdma(rows, gz_recv.at[d - 1], gz_s.at[d - 1], gz_r.at[d - 1], at_z(zz))

    def g_x(d):
        xx = (x + d) % NX
        return rdma(gx_send.at[xx], gx_recv.at[d - 1], gx_s.at[d - 1], gx_r.at[d - 1], at_x(xx))

    g_c = rdma(gc_send.at[1 - c], gc_recv, gc_s, gc_r, at_sib)

    def d_pair(i):
        return rdma(d_sib.at[i], d_sib_r.at[i], ds_s.at[i], ds_r.at[i], at_sib)

    def d_far(i):
        return rdma(d_x.at[i], d_x_r.at[i], dx_s.at[i], dx_r.at[i], at_far)

    def each(count, step):
        def body(i, carry):
            step(i)
            return carry

        lax.fori_loop(0, count, body, 0)

    w_send[...] = jnp.zeros_like(w_send)
    w_send[0:DEV_ROWS] = w_own[:, other].astype(F32)
    pair_copy.start()

    def start_kv(i):
        kv_far(i).start()
        kv_sib(i).start()

    each(AHEAD, start_kv)
    q_copy.start()
    each(HEADS, lambda i: kv_own(i).start())

    def base_of(s):
        g = span[0, s]
        return s - jnp.where(g == 1, 0, jnp.where(g == 2, s % 2, s % 4))

    my_base = base_of(me)
    place = lax.broadcasted_iota(jnp.int32, (8, TOK), 1)
    for r, s in enumerate((me, sib, far, cross)):
        base = base_of(s)
        live = jnp.where(base == my_base, clip[0, s] - (s - base) * TOK, 0)
        bias_s[:, r * TOK : (r + 1) * TOK] = jnp.where(place < live, 0.0, FLOOR)

    pair_wait.wait_recv()
    w_tmp[...] = jnp.zeros_like(w_tmp)
    own_rows = w_own[:, mine].astype(F32)
    their_rows = jnp.where(c == 0, w_pair[1, 0:DEV_ROWS], w_pair[0, 0:DEV_ROWS])
    w_tmp[0:DEV_ROWS] = jnp.where(c == 0, own_rows, their_rows)
    w_tmp[DEV_ROWS:CHIP_ROWS] = jnp.where(c == 0, their_rows, own_rows)
    w_x[x] = w_tmp[...].astype(BF16)
    for d in range(1, NX):
        x_copy(d).start()
    for d in range(1, NX):
        x_wait(d).wait_recv()
    for k in range(NX):
        w_slab[k * CHIP_ROWS : (k + 1) * CHIP_ROWS] = w_x[k].astype(F32)[0:CHIP_ROWS]
    slab(y, z)[...] = w_slab[...].astype(BF16)
    for i in range(NZ - 1):
        z_copy(z_order(i)).start()
    y_copy(0, 0).start()
    y_copy(0, 1).start()

    q_copy.wait()
    each(HEADS, lambda i: kv_own(i).wait())

    def scores_of(i):
        keys = kv[i, :, :, 0:DIM].reshape(4 * TOK, DIM)
        raw = mm(q_s[head(i)], keys, NT)
        return raw * (SCALE * LOG2E) + bias_s[0:1, :]

    def o_columns(i):
        return pl.ds(pl.multiple_of(head(i) * DIM, DIM), DIM)

    def pair_sum(i):
        g_pair(i).wait_recv()
        total = g_tmp[i % 2] + g_recv[i].astype(F32)

        @pl.when(i < HEADS - OWN_HEADS)
        def _():
            k = jnp.minimum(i, HEADS - OWN_HEADS - 1)
            gy_send[k] = total.astype(BF16)
            g_y(k).start()

        @pl.when(i >= HEADS - OWN_HEADS)
        def _():
            g_acc[jnp.maximum(i - (HEADS - OWN_HEADS), 0)] = total

    def forward(i):
        @pl.when(i + AHEAD < HEADS)
        def _():
            start_kv(jnp.minimum(i + AHEAD, HEADS - 1))

        kv_far(i).wait_recv()
        kv_relay(i).start()

        @pl.when(i < NZ - 1)
        def _():
            d = z_order(jnp.minimum(i, NZ - 2))
            z_wait(d).wait_recv()
            y_copy(d, 0).start()
            y_copy(d, 1).start()

        @pl.when((i >= 1) & (i <= NZ))
        def _():
            d = jnp.where(i <= 1, 0, z_order(jnp.clip(i - 2, 0, NZ - 2)))
            y_wait(d, 0).wait_recv()
            y_wait(d, 1).wait_recv()
            y_relay(d).start()

        @pl.when(i == NZ - 1)
        def _():
            block_copy(0).start()

        @pl.when(i == NZ + 1)
        def _():
            block_copy(1).start()
            block_copy(2).start()

        @pl.when(i == NZ + 2)
        def _():
            each(NZ, lambda d: y_relay_wait(d).wait_recv())
            block_copy(3).start()

        @pl.when(i >= 1)
        def _():
            pair_sum(jnp.maximum(i - 1, 0))

        kv_sib(i).wait_recv()
        kv_relay(i).wait_recv()
        scores = scores_of(i)
        top = jnp.max(scores, axis=1, keepdims=True)
        weights = jnp.exp2(scores - top)
        total = jnp.sum(weights, axis=1, keepdims=True)
        lse_s[i] = top + jnp.log2(total)
        probs = (weights * (1.0 / total)).astype(BF16)
        values = kv[i, :, :, DIM:].reshape(4 * TOK, DIM)
        attended = mm(probs, values, NN).astype(BF16)
        o_s[:, o_columns(i)] = attended
        g_send[i] = mm(attended, gp[0, :, other], TN).astype(BF16)
        g_pair(i).start()
        g_tmp[i % 2] = mm(attended, gp[0, :, mine], TN)

    each(HEADS, forward)
    pair_sum(HEADS - 1)
    for k in range(4):
        block_wait(k).wait_recv()

    def far_send(i):
        d_pair(i).wait_recv()
        d_x[i] = (d_rs[i % 2] + d_sib_r[i, 1].astype(F32)).astype(BF16)
        d_far(i).start()

    def backward(i):
        @pl.when(i >= 1)
        def _():
            far_send(jnp.maximum(i - 1, 0))

        @pl.when(i == 2)
        def _():
            each(HEADS - OWN_HEADS, lambda k: g_y(k).wait_recv())
            for k in range(OWN_HEADS):
                total = g_acc[k]
                for source in range(NY - 1):
                    total = total + gy_recv[source * OWN_HEADS + k].astype(F32)
                g_acc[k] = total
                gz_send[k * DIM : (k + 1) * DIM] = total.astype(BF16)
            for d in range(1, NZ):
                g_z(d).start()

        h = head(i)
        w_head = w_all[pl.ds(pl.multiple_of(h * DIM, DIM), DIM), :]
        grad_att = mm(gp[0], w_head, NT).astype(BF16)
        delta = jnp.sum(grad_att.astype(F32) * o_s[:, o_columns(i)].astype(F32), axis=1, keepdims=True)
        probs = jnp.exp2(scores_of(i) - lse_s[i])
        values = kv[i, :, :, DIM:].reshape(4 * TOK, DIM)
        dprobs = mm(grad_att, values, NT)
        dscores = (probs * (dprobs - delta)).astype(BF16)
        probs_b = probs.astype(BF16)
        keys = kv[i, :, :, 0:DIM].reshape(4 * TOK, DIM)
        grad_o[0, h, :, 0:DIM] = (mm(dscores, keys, NN) * SCALE).astype(BF16)
        dk = mm(dscores, q_s[h], TN) * SCALE
        dv = mm(probs_b, grad_att, TN)
        d_own[i, :, 0:DIM] = dk[0:TOK]
        d_own[i, :, DIM:] = dv[0:TOK]
        d_sib[i, 0, :, 0:DIM] = dk[TOK : 2 * TOK].astype(BF16)
        d_sib[i, 0, :, DIM:] = dv[TOK : 2 * TOK].astype(BF16)
        d_sib[i, 1, :, 0:DIM] = dk[3 * TOK :].astype(BF16)
        d_sib[i, 1, :, DIM:] = dv[3 * TOK :].astype(BF16)
        d_pair(i).start()
        d_rs[i % 2, :, 0:DIM] = dk[2 * TOK : 3 * TOK]
        d_rs[i % 2, :, DIM:] = dv[2 * TOK : 3 * TOK]

    each(HEADS, backward)
    far_send(HEADS - 1)

    def project(k):
        columns = pl.ds(pl.multiple_of(k * TOK, TOK), TOK)
        proj_o[0, :, columns] = mm(o_s[...], w_all[:, columns], NN).astype(BF16)

    each(WIDTH // TOK, project)

    def finish(i):
        d_far(i).wait_recv()
        total = d_own[i] + d_sib_r[i, 0].astype(F32) + d_x_r[i].astype(F32)
        grad_o[0, head(i), :, DIM:] = total.astype(BF16)

    each(3, finish)

    for d in range(1, NZ):
        g_z(d).wait_recv()
    acc = g_acc.reshape(BLOCK, HALF)
    total = acc[pl.ds(pl.multiple_of(SLAB * z, 8), SLAB)]
    for d in range(1, NZ):
        total = total + gz_recv[d - 1].astype(F32)
    gx_in[...] = total
    for k in range(NX):
        gx_send[k] = jnp.zeros_like(gx_send[k])
        gx_send[k, 0:CHIP_ROWS] = gx_in[k * CHIP_ROWS : (k + 1) * CHIP_ROWS]
    for d in range(1, NX):
        g_x(d).start()

    each(3, lambda i: finish(i + 3))

    for d in range(1, NX):
        g_x(d).wait_recv()
    total = gx_send[x]
    for d in range(1, NX):
        total = total + gx_recv[d - 1]
    for k in range(2):
        gc_send[k] = jnp.zeros_like(gc_send[k])
        gc_send[k, 0:DEV_ROWS] = total[k * DEV_ROWS : (k + 1) * DEV_ROWS]
    g_c.start()

    each(HEADS - 6, lambda i: finish(i + 6))

    g_c.wait_recv()
    gw_o[:, mine] = gc_send[c, 0:DEV_ROWS]
    gw_o[:, other] = gc_recv[0:DEV_ROWS]

    def sent(i):
        kv_far(i).wait_send()
        kv_sib(i).wait_send()
        kv_relay(i).wait_send()
        g_pair(i).wait_send()
        d_pair(i).wait_send()
        d_far(i).wait_send()

    each(HEADS, sent)
    each(HEADS - OWN_HEADS, lambda i: g_y(i).wait_send())
    pair_copy.wait_send()
    g_c.wait_send()
    for d in range(1, NX):
        x_copy(d).wait_send()
        g_x(d).wait_send()
    for d in range(1, NZ):
        z_copy(d).wait_send()
        g_z(d).wait_send()

    def sent_y(d):
        y_copy(d, 0).wait_send()
        y_copy(d, 1).wait_send()
        y_relay(d).wait_send()

    each(NZ, sent_y)
    for k in range(4):
        block_copy(k).wait_send()


def local(qkv, out_weight, grad_projected, group_span, clip_length):
    vmem = functools.partial(pl.BlockSpec, memory_space=pltpu.VMEM)
    smem = functools.partial(pl.BlockSpec, memory_space=pltpu.SMEM)
    sem = pltpu.SemaphoreType.DMA
    scratch = [
        pltpu.VMEM((HEADS, TOK, DIM), BF16),
        pltpu.VMEM((HEADS, 4, TOK, 2 * DIM), BF16),
        pltpu.VMEM((8, 4 * TOK), F32),
        pltpu.VMEM((WIDTH, WIDTH), BF16),
        pltpu.VMEM((TOK, WIDTH), BF16),
        pltpu.VMEM((HEADS, TOK, 1), F32),
        pltpu.VMEM((8, HALF), F32),
        pltpu.VMEM((2, 8, HALF), F32),
        pltpu.VMEM((16, HALF), F32),
        pltpu.VMEM((NX, 16, HALF), BF16),
        pltpu.VMEM((SLAB, HALF), F32),
        pltpu.VMEM((2, DIM, HALF), F32),
        pltpu.VMEM((OWN_HEADS, DIM, HALF), F32),
        pltpu.VMEM((HEADS, DIM, HALF), BF16),
        pltpu.VMEM((HEADS, DIM, HALF), BF16),
        pltpu.VMEM((HEADS - OWN_HEADS, DIM, HALF), BF16),
        pltpu.VMEM((HEADS - OWN_HEADS, DIM, HALF), BF16),
        pltpu.VMEM((BLOCK, HALF), BF16),
        pltpu.VMEM((NZ - 1, SLAB, HALF), BF16),
        pltpu.VMEM((SLAB, HALF), F32),
        pltpu.VMEM((NX, 16, HALF), F32),
        pltpu.VMEM((NX - 1, 16, HALF), F32),
        pltpu.VMEM((2, 8, HALF), F32),
        pltpu.VMEM((8, HALF), F32),
        pltpu.VMEM((HEADS, TOK, 2 * DIM), F32),
        pltpu.VMEM((2, TOK, 2 * DIM), F32),
        pltpu.VMEM((HEADS, 2, TOK, 2 * DIM), BF16),
        pltpu.VMEM((HEADS, 2, TOK, 2 * DIM), BF16),
        pltpu.VMEM((HEADS, TOK, 2 * DIM), BF16),
        pltpu.VMEM((HEADS, TOK, 2 * DIM), BF16),
        sem((1 + HEADS,)),
        sem((HEADS,)), sem((HEADS,)),
        sem((HEADS,)), sem((HEADS,)),
        sem((HEADS,)), sem((HEADS,)),
        sem, sem,
        sem((NX - 1,)), sem((NX - 1,)),
        sem((NZ - 1,)), sem((NZ - 1,)),
        sem((NZ, 2)), sem((NZ, 2)),
        sem((NZ,)), sem((NZ,)),
        sem((4,)), sem((4,)),
        sem((HEADS,)), sem((HEADS,)),
        sem((HEADS - OWN_HEADS,)), sem((HEADS - OWN_HEADS,)),
        sem((NZ - 1,)), sem((NZ - 1,)),
        sem((NX - 1,)), sem((NX - 1,)),
        sem, sem,
        sem((HEADS,)), sem((HEADS,)),
        sem((HEADS,)), sem((HEADS,)),
    ]
    return pl.pallas_call(
        kernel,
        out_shape=(
            jax.ShapeDtypeStruct((1, TOK, WIDTH), BF16),
            jax.ShapeDtypeStruct((1, HEADS, TOK, 3 * DIM), BF16),
            jax.ShapeDtypeStruct((DEV_ROWS, WIDTH), F32),
        ),
        in_specs=[pl.BlockSpec(memory_space=pl.ANY), vmem(), vmem(), smem(), smem()],
        out_specs=(vmem(), vmem(), vmem()),
        scratch_shapes=scratch,
        compiler_params=pltpu.CompilerParams(
            collective_id=0, has_side_effects=True, vmem_limit_bytes=60 * 1024 * 1024
        ),
        cost_estimate=pl.CostEstimate(flops=10**10, bytes_accessed=10**7, transcendentals=7 * 10**6),
    )(qkv, out_weight, grad_projected, group_span, clip_length)


def solution(mesh):
    in_specs = (
        P("dp", None, "seq", None),
        P(("dp", "seq"), None),
        P("dp", "seq", None),
        P("dp", None),
        P("dp", None),
    )
    out_specs = (P("dp", "seq", None), P("dp", None, "seq", None), P(("dp", "seq"), None))
    return jax.shard_map(local, mesh=mesh, in_specs=in_specs, out_specs=out_specs, check_vma=False)
```

```python
import functools

import jax
import jax.numpy as jnp
from jax import lax
from jax.experimental import pallas as pl
from jax.experimental.pallas import tpu as pltpu
from jax.sharding import PartitionSpec as P

HEADS = 12
DIM = 128
TOK = 256
WIDTH = 1536
HALF = WIDTH // 2
QUARTER = HALF // 2
NY = 4
NZ = 8
NX = 4
SLAB = 48
BLOCK = SLAB * NZ
OWN_HEADS = HEADS // NY
CHIP_ROWS = 12
DEV_ROWS = 6
AHEAD = 4
LAG = 9
WEIGHT_PASS = {1: (0, 1), 2: (2, 3), 3: (4, 5), 4: (6,)}
WEIGHT_RELAY = {1: (0,), 3: (1, 2), 4: (3, 4), 5: (5, 6), 6: (7,)}
WEIGHT_OWN, WEIGHT_NEAR, WEIGHT_LAST = 5, 7, 12
G_AT = (8, 10, 11)
GZ_AT = 16
FLOOR = -1e30
SCALE = DIM**-0.5
LOG2E = 1.4426950408889634
MESH = pl.DeviceIdType.MESH
F32 = jnp.float32
BF16 = jnp.bfloat16


def mm(a, b, dims):
    return lax.dot_general(a, b, (dims, ((), ())), preferred_element_type=F32)


NN = ((1,), (0,))
NT = ((1,), (1,))
TN = ((0,), (0,))


def kernel(
    qkv, w_own, gp, span, clip,
    proj_o, grad_o, gw_o,
    q_s, kv, bias_s, w_all, o_s, lse_s,
    w_send, w_pair, w_tmp, w_x, w_slab,
    g_own, g_acc, g_send, g_recv, gy_send, gr_recv, gy_recv, gz_send, gz_recv,
    gx_in, gx_send, gx_recv, gc_send, gc_recv,
    d_own, d_rs, d_sib, d_sib_r, d_x, d_x_r,
    loc_sem, ks_s, ks_r, kx_s, kx_r, kf_s, kf_r,
    wa_s, wa_r, wx_s, wx_r, wz_s, wz_r, wy_s, wy_r, wf_s, wf_r, wb_s, wb_r,
    gs_s, gs_r, gr_s, gr_r, gy_s, gy_r, gz_s, gz_r, gx_s, gx_r, gc_s, gc_r,
    ds_s, ds_r, dx_s, dx_r,
):
    me = lax.axis_index("seq")
    y = lax.axis_index("dp")
    c = me % 2
    x = (me // 2) % NX
    z = me // (2 * NX)
    sib = me + 1 - 2 * c
    far = me + 2 - 4 * (x % 2)
    cross = far + 1 - 2 * c

    def at_x(xx):
        return {"seq": (z * NX + xx) * 2 + c}

    def at_z(zz):
        return {"seq": (zz * NX + x) * 2 + c}

    def at_y(yy):
        return {"dp": yy}

    at_sib = {"seq": sib}
    at_far = {"seq": far}

    def rdma(src, dst, send, recv, device):
        return pltpu.make_async_remote_copy(
            src_ref=src, dst_ref=dst, send_sem=send, recv_sem=recv,
            device_id=device, device_id_type=MESH,
        )

    partners = [at_sib]
    partners += [at_x((x + d) % NX) for d in range(1, NX)]
    partners += [at_z((z + d) % NZ) for d in range(1, NZ)]
    partners += [at_y((y + 1) % NY), at_y((y + NY - 1) % NY)]
    barrier = pltpu.get_barrier_semaphore()
    for partner in partners:
        pl.semaphore_signal(barrier, inc=1, device_id=partner, device_id_type=MESH)
    pl.semaphore_wait(barrier, len(partners))

    def head(i):
        part = i // OWN_HEADS
        owner = y + jnp.where(part == 0, 2, jnp.where(part == 1, 1, jnp.where(part == 2, 3, 0)))
        return (OWN_HEADS * owner + i % OWN_HEADS) % HEADS

    def back_order(b):
        return OWN_HEADS * (NY - 1 - b // OWN_HEADS) + b % OWN_HEADS

    def kv_sib(i):
        return rdma(qkv.at[0, head(i), :, pl.ds(DIM, 2 * DIM)], kv.at[i, 1], ks_s.at[i], ks_r.at[i], at_sib)

    def kv_far(i):
        return rdma(qkv.at[0, head(i), :, pl.ds(DIM, 2 * DIM)], kv.at[i, 2], kx_s.at[i], kx_r.at[i], at_far)

    def kv_relay(i):
        return rdma(kv.at[i, 2], kv.at[i, 3], kf_s.at[i], kf_r.at[i], at_sib)

    def kv_own(i):
        return pltpu.make_async_copy(qkv.at[0, head(i), :, pl.ds(DIM, 2 * DIM)], kv.at[i, 0], loc_sem.at[1 + i])

    q_copy = pltpu.make_async_copy(qkv.at[0, :, :, pl.ds(0, DIM)], q_s, loc_sem.at[0])

    mine = pl.ds(pl.multiple_of(c * HALF, HALF), HALF)
    other = pl.ds(pl.multiple_of((1 - c) * HALF, HALF), HALF)

    def slab(yy, zz):
        return w_all.at[pl.ds(pl.multiple_of(SLAB * (NZ * yy + zz), 16), SLAB), mine]

    pair_copy = rdma(w_send, w_pair.at[c], wa_s, wa_r, at_sib)
    pair_wait = rdma(w_send, w_pair.at[1 - c], wa_s, wa_r, at_sib)

    def x_copy(d):
        return rdma(w_x.at[x], w_x.at[x], wx_s.at[d - 1], wx_r.at[d - 1], at_x((x + d) % NX))

    def x_wait(d):
        back = (x + NX - d) % NX
        return rdma(w_x.at[back], w_x.at[back], wx_s.at[d - 1], wx_r.at[d - 1], at_x(back))

    def z_copy(d):
        return rdma(slab(y, z), slab(y, z), wz_s.at[d - 1], wz_r.at[d - 1], at_z((z + d) % NZ))

    def z_wait(d):
        back = (z + NZ - d) % NZ
        return rdma(slab(y, back), slab(y, back), wz_s.at[d - 1], wz_r.at[d - 1], at_z(back))

    up, down = (y + 1) % NY, (y + NY - 1) % NY
    opposite = (y + 2) % NY

    def y_copy(d, way):
        zz = (z + NZ - d) % NZ
        return rdma(slab(y, zz), slab(y, zz), wy_s.at[d, way], wy_r.at[d, way], at_y(up if way == 0 else down))

    def y_wait(d, way):
        zz = (z + NZ - d) % NZ
        yy = down if way == 0 else up
        return rdma(slab(yy, zz), slab(yy, zz), wy_s.at[d, way], wy_r.at[d, way], at_y(yy))

    def y_relay(d):
        zz = (z + NZ - d) % NZ
        odd = d % 2
        yy = (y + NY - 1 + 2 * odd) % NY
        to = (y + 1 + 2 * odd) % NY
        return rdma(slab(yy, zz), slab(yy, zz), wf_s.at[d], wf_r.at[d], at_y(to))

    def y_relay_wait(d):
        zz = (z + NZ - d) % NZ
        return rdma(slab(opposite, zz), slab(opposite, zz), wf_s.at[d], wf_r.at[d], at_y(up))

    def rows_block(yy, columns):
        return w_all.at[pl.ds(pl.multiple_of(BLOCK * yy, 16), BLOCK), columns]

    def block_copy(k):
        yy = (y, down, up, opposite)[k]
        return rdma(rows_block(yy, mine), rows_block(yy, mine), wb_s.at[k], wb_r.at[k], at_sib)

    def block_wait(k):
        yy = (y, down, up, opposite)[k]
        return rdma(rows_block(yy, other), rows_block(yy, other), wb_s.at[k], wb_r.at[k], at_sib)

    def z_order(i):
        return 1 + i // 2 + (i % 2) * (NZ - 2 - 2 * (i // 2))

    def g_pair(i):
        return rdma(g_send.at[i], g_recv.at[i], gs_s.at[i], gs_r.at[i], at_sib)

    def g_half(k, way):
        columns = pl.ds(way * QUARTER, QUARTER)
        to = at_y(up if way == 0 else down)
        return rdma(gy_send.at[k, :, columns], gr_recv.at[way, k], gr_s.at[k, way], gr_r.at[k, way], to)

    def g_y(k, way):
        to = at_y(up if way == 0 else down)
        return rdma(gy_send.at[OWN_HEADS * (1 + way) + k], gy_recv.at[way, k], gy_s.at[k, way], gy_r.at[k, way], to)

    def g_z(d):
        zz = (z + d) % NZ
        rows = gz_send.at[pl.ds(pl.multiple_of(SLAB * zz, 16), SLAB)]
        return rdma(rows, gz_recv.at[d - 1], gz_s.at[d - 1], gz_r.at[d - 1], at_z(zz))

    def g_x(d):
        xx = (x + d) % NX
        return rdma(gx_send.at[xx], gx_recv.at[d - 1], gx_s.at[d - 1], gx_r.at[d - 1], at_x(xx))

    g_c = rdma(gc_send.at[1 - c], gc_recv, gc_s, gc_r, at_sib)

    def d_pair(i):
        return rdma(d_sib.at[i], d_sib_r.at[i], ds_s.at[i], ds_r.at[i], at_sib)

    def d_far(i):
        return rdma(d_x.at[i], d_x_r.at[i], dx_s.at[i], dx_r.at[i], at_far)

    def each(count, step):
        def body(i, carry):
            step(i)
            return carry

        lax.fori_loop(0, count, body, 0)

    w_send[...] = jnp.zeros_like(w_send)
    w_send[0:DEV_ROWS] = w_own[:, other].astype(F32)
    pair_copy.start()

    def start_kv(i):
        kv_far(i).start()
        kv_sib(i).start()

    each(AHEAD, start_kv)
    q_copy.start()
    each(HEADS, lambda i: kv_own(i).start())

    def base_of(s):
        g = span[0, s]
        return s - jnp.where(g == 1, 0, jnp.where(g == 2, s % 2, s % 4))

    my_base = base_of(me)
    place = lax.broadcasted_iota(jnp.int32, (8, TOK), 1)
    for r, s in enumerate((me, sib, far, cross)):
        base = base_of(s)
        live = jnp.where(base == my_base, clip[0, s] - (s - base) * TOK, 0)
        bias_s[:, r * TOK : (r + 1) * TOK] = jnp.where(place < live, 0.0, FLOOR)

    pair_wait.wait_recv()
    w_tmp[...] = jnp.zeros_like(w_tmp)
    own_rows = w_own[:, mine].astype(F32)
    their_rows = jnp.where(c == 0, w_pair[1, 0:DEV_ROWS], w_pair[0, 0:DEV_ROWS])
    w_tmp[0:DEV_ROWS] = jnp.where(c == 0, own_rows, their_rows)
    w_tmp[DEV_ROWS:CHIP_ROWS] = jnp.where(c == 0, their_rows, own_rows)
    w_x[x] = w_tmp[...].astype(BF16)
    for d in range(1, NX):
        x_copy(d).start()
    for d in range(1, NX):
        x_wait(d).wait_recv()
    for k in range(NX):
        w_slab[k * CHIP_ROWS : (k + 1) * CHIP_ROWS] = w_x[k].astype(F32)[0:CHIP_ROWS]
    slab(y, z)[...] = w_slab[...].astype(BF16)
    for i in range(NZ - 1):
        z_copy(z_order(i)).start()
    y_copy(0, 0).start()
    y_copy(0, 1).start()

    q_copy.wait()
    each(HEADS, lambda i: kv_own(i).wait())

    def scores_of(i):
        keys = kv[i, :, :, 0:DIM].reshape(4 * TOK, DIM)
        raw = mm(q_s[head(i)], keys, NT)
        return raw * (SCALE * LOG2E) + bias_s[0:1, :]

    def o_columns(i):
        return pl.ds(pl.multiple_of(head(i) * DIM, DIM), DIM)

    def pair_sum(i):
        g_pair(i).wait_recv()
        return g_own[i] + g_recv[i].astype(F32)

    def g_stage(part):
        def opposite_head(k):
            gy_send[k] = pair_sum(k).astype(BF16)
            g_half(k, 0).start()
            g_half(k, 1).start()

        def next_head(way, k):
            i = OWN_HEADS * (1 + way) + k
            total = pair_sum(i)
            g_half(k, way).wait_recv()
            here = slice(way * QUARTER, (way + 1) * QUARTER)
            there = slice((1 - way) * QUARTER, (2 - way) * QUARTER)
            gy_send[i, :, there] = total[:, there].astype(BF16)
            gy_send[i, :, here] = (total[:, here] + gr_recv[way, k].astype(F32)).astype(BF16)
            g_y(k, way).start()

        def own_head(k):
            g_acc[k] = pair_sum(3 * OWN_HEADS + k)

        steps = (
            opposite_head,
            functools.partial(next_head, 0),
            functools.partial(next_head, 1),
            own_head,
        )
        each(OWN_HEADS, steps[part])

    def arrive(i):
        @pl.when(i + AHEAD < HEADS)
        def _():
            start_kv(jnp.minimum(i + AHEAD, HEADS - 1))

        kv_far(i).wait_recv()
        kv_relay(i).start()

    def forward(i):
        kv_sib(i).wait_recv()
        kv_relay(i).wait_recv()
        scores = scores_of(i)
        top = jnp.max(scores, axis=1, keepdims=True)
        weights = jnp.exp2(scores - top)
        total = jnp.sum(weights, axis=1, keepdims=True)
        lse_s[i] = top + jnp.log2(total)
        probs = (weights * (1.0 / total)).astype(BF16)
        values = kv[i, :, :, DIM:].reshape(4 * TOK, DIM)
        attended = mm(probs, values, NN).astype(BF16)
        o_s[:, o_columns(i)] = attended
        g_send[i] = mm(attended, gp[0, :, other], TN).astype(BF16)
        g_pair(i).start()
        g_own[i] = mm(attended, gp[0, :, mine], TN)

    def far_send(i):
        d_pair(i).wait_recv()
        d_x[i] = (d_rs[i % 2] + d_sib_r[i, 1].astype(F32)).astype(BF16)
        d_far(i).start()

    def backward(b):
        i = back_order(b)

        @pl.when(b >= 1)
        def _():
            far_send(jnp.maximum(b - 1, 0))

        h = head(i)
        w_head = w_all[pl.ds(pl.multiple_of(h * DIM, DIM), DIM), :]
        grad_att = mm(gp[0], w_head, NT).astype(BF16)
        delta = jnp.sum(grad_att.astype(F32) * o_s[:, o_columns(i)].astype(F32), axis=1, keepdims=True)
        probs = jnp.exp2(scores_of(i) - lse_s[i])
        values = kv[i, :, :, DIM:].reshape(4 * TOK, DIM)
        dprobs = mm(grad_att, values, NT)
        dscores = (probs * (dprobs - delta)).astype(BF16)
        probs_b = probs.astype(BF16)
        keys = kv[i, :, :, 0:DIM].reshape(4 * TOK, DIM)
        grad_o[0, h, :, 0:DIM] = (mm(dscores, keys, NN) * SCALE).astype(BF16)
        dk = mm(dscores, q_s[h], TN) * SCALE
        dv = mm(probs_b, grad_att, TN)
        d_own[b, :, 0:DIM] = dk[0:TOK]
        d_own[b, :, DIM:] = dv[0:TOK]
        d_sib[b, 0, :, 0:DIM] = dk[TOK : 2 * TOK].astype(BF16)
        d_sib[b, 0, :, DIM:] = dv[TOK : 2 * TOK].astype(BF16)
        d_sib[b, 1, :, 0:DIM] = dk[3 * TOK :].astype(BF16)
        d_sib[b, 1, :, DIM:] = dv[3 * TOK :].astype(BF16)
        d_pair(b).start()
        d_rs[b % 2, :, 0:DIM] = dk[2 * TOK : 3 * TOK]
        d_rs[b % 2, :, DIM:] = dv[2 * TOK : 3 * TOK]

    def pass_slab(n):
        d = z_order(n)
        z_wait(d).wait_recv()
        y_copy(d, 0).start()
        y_copy(d, 1).start()

    def relay_slab(d):
        y_wait(d, 0).wait_recv()
        y_wait(d, 1).wait_recv()
        y_relay(d).start()

    def weight_step(t):
        for n in WEIGHT_PASS.get(t, ()):
            pass_slab(n)
        for n in WEIGHT_RELAY.get(t, ()):
            relay_slab(0 if n == 0 else z_order(n - 1))
        if t == WEIGHT_OWN:
            block_copy(0).start()
        if t == WEIGHT_NEAR:
            block_copy(1).start()
            block_copy(2).start()
        if t == WEIGHT_LAST:
            for d in range(NZ):
                y_relay_wait(d).wait_recv()
            block_copy(3).start()

    def own_sum():
        g_stage(3)
        for k in range(OWN_HEADS):
            g_y(k, 0).wait_recv()
            g_y(k, 1).wait_recv()
            total = g_acc[k] + gy_recv[0, k].astype(F32) + gy_recv[1, k].astype(F32)
            g_acc[k] = total
            gz_send[k * DIM : (k + 1) * DIM] = total.astype(BF16)
        for d in range(1, NZ):
            g_z(d).start()

    def step(t):
        @pl.when(t < HEADS)
        def _():
            i = jnp.minimum(t, HEADS - 1)
            arrive(i)

        for at in range(WEIGHT_LAST + 1):

            @pl.when(t == at)
            def _(at=at):
                weight_step(at)

        for part, at in enumerate(G_AT):

            @pl.when(t == at)
            def _(part=part):
                g_stage(part)

        @pl.when(t == GZ_AT)
        def _():
            own_sum()

        for k in range(4):

            @pl.when(t == LAG + OWN_HEADS * k)
            def _(k=k):
                block_wait(k).wait_recv()

        @pl.when(t < HEADS)
        def _():
            forward(jnp.minimum(t, HEADS - 1))

        @pl.when(t >= LAG)
        def _():
            backward(jnp.maximum(t - LAG, 0))

    each(HEADS + LAG, step)
    far_send(HEADS - 1)

    def project(k):
        columns = pl.ds(pl.multiple_of(k * TOK, TOK), TOK)
        proj_o[0, :, columns] = mm(o_s[...], w_all[:, columns], NN).astype(BF16)

    each(WIDTH // TOK, project)

    def finish(i):
        d_far(i).wait_recv()
        total = d_own[i] + d_sib_r[i, 0].astype(F32) + d_x_r[i].astype(F32)
        grad_o[0, head(back_order(i)), :, DIM:] = total.astype(BF16)

    each(3, finish)

    for d in range(1, NZ):
        g_z(d).wait_recv()
    acc = g_acc.reshape(BLOCK, HALF)
    total = acc[pl.ds(pl.multiple_of(SLAB * z, 8), SLAB)]
    for d in range(1, NZ):
        total = total + gz_recv[d - 1].astype(F32)
    gx_in[...] = total
    for k in range(NX):
        gx_send[k] = jnp.zeros_like(gx_send[k])
        gx_send[k, 0:CHIP_ROWS] = gx_in[k * CHIP_ROWS : (k + 1) * CHIP_ROWS]
    for d in range(1, NX):
        g_x(d).start()

    each(3, lambda i: finish(i + 3))

    for d in range(1, NX):
        g_x(d).wait_recv()
    total = gx_send[x]
    for d in range(1, NX):
        total = total + gx_recv[d - 1]
    for k in range(2):
        gc_send[k] = jnp.zeros_like(gc_send[k])
        gc_send[k, 0:DEV_ROWS] = total[k * DEV_ROWS : (k + 1) * DEV_ROWS]
    g_c.start()

    each(HEADS - 6, lambda i: finish(i + 6))

    g_c.wait_recv()
    gw_o[:, mine] = gc_send[c, 0:DEV_ROWS]
    gw_o[:, other] = gc_recv[0:DEV_ROWS]

    def sent(i):
        kv_far(i).wait_send()
        kv_sib(i).wait_send()
        kv_relay(i).wait_send()
        g_pair(i).wait_send()
        d_pair(i).wait_send()
        d_far(i).wait_send()

    each(HEADS, sent)

    def sent_g(k):
        for way in range(2):
            g_half(k, way).wait_send()
            g_y(k, way).wait_send()

    each(OWN_HEADS, sent_g)
    pair_copy.wait_send()
    g_c.wait_send()
    for d in range(1, NX):
        x_copy(d).wait_send()
        g_x(d).wait_send()
    for d in range(1, NZ):
        z_copy(d).wait_send()
        g_z(d).wait_send()

    def sent_y(d):
        y_copy(d, 0).wait_send()
        y_copy(d, 1).wait_send()
        y_relay(d).wait_send()

    each(NZ, sent_y)
    for k in range(4):
        block_copy(k).wait_send()


def local(qkv, out_weight, grad_projected, group_span, clip_length):
    vmem = functools.partial(pl.BlockSpec, memory_space=pltpu.VMEM)
    smem = functools.partial(pl.BlockSpec, memory_space=pltpu.SMEM)
    sem = pltpu.SemaphoreType.DMA
    scratch = [
        pltpu.VMEM((HEADS, TOK, DIM), BF16),
        pltpu.VMEM((HEADS, 4, TOK, 2 * DIM), BF16),
        pltpu.VMEM((8, 4 * TOK), F32),
        pltpu.VMEM((WIDTH, WIDTH), BF16),
        pltpu.VMEM((TOK, WIDTH), BF16),
        pltpu.VMEM((HEADS, TOK, 1), F32),
        pltpu.VMEM((8, HALF), F32),
        pltpu.VMEM((2, 8, HALF), F32),
        pltpu.VMEM((16, HALF), F32),
        pltpu.VMEM((NX, 16, HALF), BF16),
        pltpu.VMEM((SLAB, HALF), F32),
        pltpu.VMEM((HEADS, DIM, HALF), F32),
        pltpu.VMEM((OWN_HEADS, DIM, HALF), F32),
        pltpu.VMEM((HEADS, DIM, HALF), BF16),
        pltpu.VMEM((HEADS, DIM, HALF), BF16),
        pltpu.VMEM((HEADS - OWN_HEADS, DIM, HALF), BF16),
        pltpu.VMEM((2, OWN_HEADS, DIM, QUARTER), BF16),
        pltpu.VMEM((2, OWN_HEADS, DIM, HALF), BF16),
        pltpu.VMEM((BLOCK, HALF), BF16),
        pltpu.VMEM((NZ - 1, SLAB, HALF), BF16),
        pltpu.VMEM((SLAB, HALF), F32),
        pltpu.VMEM((NX, 16, HALF), F32),
        pltpu.VMEM((NX - 1, 16, HALF), F32),
        pltpu.VMEM((2, 8, HALF), F32),
        pltpu.VMEM((8, HALF), F32),
        pltpu.VMEM((HEADS, TOK, 2 * DIM), F32),
        pltpu.VMEM((2, TOK, 2 * DIM), F32),
        pltpu.VMEM((HEADS, 2, TOK, 2 * DIM), BF16),
        pltpu.VMEM((HEADS, 2, TOK, 2 * DIM), BF16),
        pltpu.VMEM((HEADS, TOK, 2 * DIM), BF16),
        pltpu.VMEM((HEADS, TOK, 2 * DIM), BF16),
        sem((1 + HEADS,)),
        sem((HEADS,)), sem((HEADS,)),
        sem((HEADS,)), sem((HEADS,)),
        sem((HEADS,)), sem((HEADS,)),
        sem, sem,
        sem((NX - 1,)), sem((NX - 1,)),
        sem((NZ - 1,)), sem((NZ - 1,)),
        sem((NZ, 2)), sem((NZ, 2)),
        sem((NZ,)), sem((NZ,)),
        sem((4,)), sem((4,)),
        sem((HEADS,)), sem((HEADS,)),
        sem((OWN_HEADS, 2)), sem((OWN_HEADS, 2)),
        sem((OWN_HEADS, 2)), sem((OWN_HEADS, 2)),
        sem((NZ - 1,)), sem((NZ - 1,)),
        sem((NX - 1,)), sem((NX - 1,)),
        sem, sem,
        sem((HEADS,)), sem((HEADS,)),
        sem((HEADS,)), sem((HEADS,)),
    ]
    return pl.pallas_call(
        kernel,
        out_shape=(
            jax.ShapeDtypeStruct((1, TOK, WIDTH), BF16),
            jax.ShapeDtypeStruct((1, HEADS, TOK, 3 * DIM), BF16),
            jax.ShapeDtypeStruct((DEV_ROWS, WIDTH), F32),
        ),
        in_specs=[pl.BlockSpec(memory_space=pl.ANY), vmem(), vmem(), smem(), smem()],
        out_specs=(vmem(), vmem(), vmem()),
        scratch_shapes=scratch,
        compiler_params=pltpu.CompilerParams(
            collective_id=0, has_side_effects=True, vmem_limit_bytes=60 * 1024 * 1024
        ),
        cost_estimate=pl.CostEstimate(flops=10**10, bytes_accessed=10**7, transcendentals=7 * 10**6),
    )(qkv, out_weight, grad_projected, group_span, clip_length)


def solution(mesh):
    in_specs = (
        P("dp", None, "seq", None),
        P(("dp", "seq"), None),
        P("dp", "seq", None),
        P("dp", None),
        P("dp", None),
    )
    out_specs = (P("dp", "seq", None), P("dp", None, "seq", None), P(("dp", "seq"), None))
    return jax.shard_map(local, mesh=mesh, in_specs=in_specs, out_specs=out_specs, check_vma=False)
```

```python
import functools

import jax
import jax.numpy as jnp
from jax import lax
from jax.experimental import pallas as pl
from jax.experimental.pallas import tpu as pltpu
from jax.sharding import PartitionSpec as P

HEADS = 12
DIM = 128
TOK = 256
WIDTH = 1536
HALF = WIDTH // 2
QUARTER = HALF // 2
NY = 4
NZ = 8
NX = 4
SLAB = 48
BLOCK = SLAB * NZ
OWN_HEADS = HEADS // NY
CHIP_ROWS = 12
DEV_ROWS = 6
AHEAD = 2
LAG = 9
WEIGHT_SEND = {0: (2, 3), 1: (4, 5), 2: (6,)}
WEIGHT_PASS = {2: (0, 1), 3: (2, 3), 4: (4, 5), 5: (6,)}
WEIGHT_RELAY = {2: (0,), 4: (1, 2), 5: (3, 4), 6: (5, 6), 7: (7,)}
WEIGHT_OWN, WEIGHT_NEAR, WEIGHT_LAST = 6, 8, 13
G_AT = (8, 10, 11)
GZ_AT = 16
FLOOR = -1e30
SCALE = DIM**-0.5
LOG2E = 1.4426950408889634
MESH = pl.DeviceIdType.MESH
F32 = jnp.float32
BF16 = jnp.bfloat16


def mm(a, b, dims):
    return lax.dot_general(a, b, (dims, ((), ())), preferred_element_type=F32)


NN = ((1,), (0,))
NT = ((1,), (1,))
TN = ((0,), (0,))


def kernel(
    qkv, w_own, gp, span, clip,
    proj_o, grad_o, gw_o,
    q_s, kv, bias_s, w_all, o_s, lse_s,
    w_send, w_pair, w_tmp, w_x, w_slab,
    g_own, g_acc, g_send, g_recv, gy_send, gr_recv, gy_recv, gz_send, gz_recv,
    gx_in, gx_send, gx_recv, gc_send, gc_recv,
    d_own, d_rs, d_sib, d_sib_r, d_x, d_x_r,
    loc_sem, ks_s, ks_r, kx_s, kx_r, kf_s, kf_r,
    wa_s, wa_r, wx_s, wx_r, wz_s, wz_r, wy_s, wy_r, wf_s, wf_r, wb_s, wb_r,
    gs_s, gs_r, gr_s, gr_r, gy_s, gy_r, gz_s, gz_r, gx_s, gx_r, gc_s, gc_r,
    ds_s, ds_r, dx_s, dx_r,
):
    me = lax.axis_index("seq")
    y = lax.axis_index("dp")
    c = me % 2
    x = (me // 2) % NX
    z = me // (2 * NX)
    sib = me + 1 - 2 * c
    far = me + 2 - 4 * (x % 2)
    cross = far + 1 - 2 * c

    def at_x(xx):
        return {"seq": (z * NX + xx) * 2 + c}

    def at_z(zz):
        return {"seq": (zz * NX + x) * 2 + c}

    def at_y(yy):
        return {"dp": yy}

    at_sib = {"seq": sib}
    at_far = {"seq": far}

    def rdma(src, dst, send, recv, device):
        return pltpu.make_async_remote_copy(
            src_ref=src, dst_ref=dst, send_sem=send, recv_sem=recv,
            device_id=device, device_id_type=MESH,
        )

    partners = [at_sib]
    partners += [at_x((x + d) % NX) for d in range(1, NX)]
    partners += [at_z((z + d) % NZ) for d in range(1, NZ)]
    partners += [at_y((y + 1) % NY), at_y((y + NY - 1) % NY)]
    barrier = pltpu.get_barrier_semaphore()
    for partner in partners:
        pl.semaphore_signal(barrier, inc=1, device_id=partner, device_id_type=MESH)
    pl.semaphore_wait(barrier, len(partners))

    def head(i):
        part = i // OWN_HEADS
        owner = y + jnp.where(part == 0, 2, jnp.where(part == 1, 1, jnp.where(part == 2, 3, 0)))
        return (OWN_HEADS * owner + i % OWN_HEADS) % HEADS

    def back_order(b):
        return OWN_HEADS * (NY - 1 - b // OWN_HEADS) + b % OWN_HEADS

    def kv_sib(i):
        return rdma(qkv.at[0, head(i), :, pl.ds(DIM, 2 * DIM)], kv.at[i, 1], ks_s.at[i], ks_r.at[i], at_sib)

    def kv_far(i):
        return rdma(qkv.at[0, head(i), :, pl.ds(DIM, 2 * DIM)], kv.at[i, 2], kx_s.at[i], kx_r.at[i], at_far)

    def kv_relay(i):
        return rdma(kv.at[i, 2], kv.at[i, 3], kf_s.at[i], kf_r.at[i], at_sib)

    def kv_own(i):
        return pltpu.make_async_copy(qkv.at[0, head(i), :, pl.ds(DIM, 2 * DIM)], kv.at[i, 0], loc_sem.at[1 + i])

    q_copy = pltpu.make_async_copy(qkv.at[0, :, :, pl.ds(0, DIM)], q_s, loc_sem.at[0])

    mine = pl.ds(pl.multiple_of(c * HALF, HALF), HALF)
    other = pl.ds(pl.multiple_of((1 - c) * HALF, HALF), HALF)

    def slab(yy, zz):
        return w_all.at[pl.ds(pl.multiple_of(SLAB * (NZ * yy + zz), 16), SLAB), mine]

    pair_copy = rdma(w_send, w_pair.at[c], wa_s, wa_r, at_sib)
    pair_wait = rdma(w_send, w_pair.at[1 - c], wa_s, wa_r, at_sib)

    def x_copy(d):
        return rdma(w_x.at[x], w_x.at[x], wx_s.at[d - 1], wx_r.at[d - 1], at_x((x + d) % NX))

    def x_wait(d):
        back = (x + NX - d) % NX
        return rdma(w_x.at[back], w_x.at[back], wx_s.at[d - 1], wx_r.at[d - 1], at_x(back))

    def z_copy(d):
        return rdma(slab(y, z), slab(y, z), wz_s.at[d - 1], wz_r.at[d - 1], at_z((z + d) % NZ))

    def z_wait(d):
        back = (z + NZ - d) % NZ
        return rdma(slab(y, back), slab(y, back), wz_s.at[d - 1], wz_r.at[d - 1], at_z(back))

    up, down = (y + 1) % NY, (y + NY - 1) % NY
    opposite = (y + 2) % NY

    def y_copy(d, way):
        zz = (z + NZ - d) % NZ
        return rdma(slab(y, zz), slab(y, zz), wy_s.at[d, way], wy_r.at[d, way], at_y(up if way == 0 else down))

    def y_wait(d, way):
        zz = (z + NZ - d) % NZ
        yy = down if way == 0 else up
        return rdma(slab(yy, zz), slab(yy, zz), wy_s.at[d, way], wy_r.at[d, way], at_y(yy))

    def y_relay(d):
        zz = (z + NZ - d) % NZ
        odd = d % 2
        yy = (y + NY - 1 + 2 * odd) % NY
        to = (y + 1 + 2 * odd) % NY
        return rdma(slab(yy, zz), slab(yy, zz), wf_s.at[d], wf_r.at[d], at_y(to))

    def y_relay_wait(d):
        zz = (z + NZ - d) % NZ
        return rdma(slab(opposite, zz), slab(opposite, zz), wf_s.at[d], wf_r.at[d], at_y(up))

    def rows_block(yy, columns):
        return w_all.at[pl.ds(pl.multiple_of(BLOCK * yy, 16), BLOCK), columns]

    def block_copy(k):
        yy = (y, down, up, opposite)[k]
        return rdma(rows_block(yy, mine), rows_block(yy, mine), wb_s.at[k], wb_r.at[k], at_sib)

    def block_wait(k):
        yy = (y, down, up, opposite)[k]
        return rdma(rows_block(yy, other), rows_block(yy, other), wb_s.at[k], wb_r.at[k], at_sib)

    def z_order(i):
        return 1 + i // 2 + (i % 2) * (NZ - 2 - 2 * (i // 2))

    def g_pair(i):
        return rdma(g_send.at[i], g_recv.at[i], gs_s.at[i], gs_r.at[i], at_sib)

    def g_half(k, way):
        columns = pl.ds(way * QUARTER, QUARTER)
        to = at_y(up if way == 0 else down)
        return rdma(gy_send.at[k, :, columns], gr_recv.at[way, k], gr_s.at[k, way], gr_r.at[k, way], to)

    def g_y(k, way):
        to = at_y(up if way == 0 else down)
        return rdma(gy_send.at[OWN_HEADS * (1 + way) + k], gy_recv.at[way, k], gy_s.at[k, way], gy_r.at[k, way], to)

    def g_z(d):
        zz = (z + d) % NZ
        rows = gz_send.at[pl.ds(pl.multiple_of(SLAB * zz, 16), SLAB)]
        return rdma(rows, gz_recv.at[d - 1], gz_s.at[d - 1], gz_r.at[d - 1], at_z(zz))

    def g_x(d):
        xx = (x + d) % NX
        return rdma(gx_send.at[xx], gx_recv.at[d - 1], gx_s.at[d - 1], gx_r.at[d - 1], at_x(xx))

    g_c = rdma(gc_send.at[1 - c], gc_recv, gc_s, gc_r, at_sib)

    def d_pair(i):
        return rdma(d_sib.at[i], d_sib_r.at[i], ds_s.at[i], ds_r.at[i], at_sib)

    def d_far(i):
        return rdma(d_x.at[i], d_x_r.at[i], dx_s.at[i], dx_r.at[i], at_far)

    def each(count, step):
        def body(i, carry):
            step(i)
            return carry

        lax.fori_loop(0, count, body, 0)

    w_send[...] = jnp.zeros_like(w_send)
    w_send[0:DEV_ROWS] = w_own[:, other].astype(F32)
    pair_copy.start()

    def start_kv(i):
        kv_far(i).start()
        kv_sib(i).start()

    each(AHEAD, start_kv)
    q_copy.start()
    each(HEADS, lambda i: kv_own(i).start())

    def base_of(s):
        g = span[0, s]
        return s - jnp.where(g == 1, 0, jnp.where(g == 2, s % 2, s % 4))

    my_base = base_of(me)
    place = lax.broadcasted_iota(jnp.int32, (8, TOK), 1)
    for r, s in enumerate((me, sib, far, cross)):
        base = base_of(s)
        live = jnp.where(base == my_base, clip[0, s] - (s - base) * TOK, 0)
        bias_s[:, r * TOK : (r + 1) * TOK] = jnp.where(place < live, 0.0, FLOOR)

    pair_wait.wait_recv()
    w_tmp[...] = jnp.zeros_like(w_tmp)
    own_rows = w_own[:, mine].astype(F32)
    their_rows = jnp.where(c == 0, w_pair[1, 0:DEV_ROWS], w_pair[0, 0:DEV_ROWS])
    w_tmp[0:DEV_ROWS] = jnp.where(c == 0, own_rows, their_rows)
    w_tmp[DEV_ROWS:CHIP_ROWS] = jnp.where(c == 0, their_rows, own_rows)
    w_x[x] = w_tmp[...].astype(BF16)
    for d in range(1, NX):
        x_copy(d).start()
    for d in range(1, NX):
        x_wait(d).wait_recv()
    for k in range(NX):
        w_slab[k * CHIP_ROWS : (k + 1) * CHIP_ROWS] = w_x[k].astype(F32)[0:CHIP_ROWS]
    slab(y, z)[...] = w_slab[...].astype(BF16)
    for i in range(2):
        z_copy(z_order(i)).start()
    y_copy(0, 0).start()
    y_copy(0, 1).start()

    q_copy.wait()
    each(HEADS, lambda i: kv_own(i).wait())

    def scores_of(i):
        keys = kv[i, :, :, 0:DIM].reshape(4 * TOK, DIM)
        raw = mm(q_s[head(i)], keys, NT)
        return raw * (SCALE * LOG2E) + bias_s[0:1, :]

    def o_columns(i):
        return pl.ds(pl.multiple_of(head(i) * DIM, DIM), DIM)

    def pair_sum(i):
        g_pair(i).wait_recv()
        return g_own[i] + g_recv[i].astype(F32)

    def g_stage(part):
        def opposite_head(k):
            gy_send[k] = pair_sum(k).astype(BF16)
            g_half(k, 0).start()
            g_half(k, 1).start()

        def next_head(way, k):
            i = OWN_HEADS * (1 + way) + k
            total = pair_sum(i)
            g_half(k, way).wait_recv()
            here = slice(way * QUARTER, (way + 1) * QUARTER)
            there = slice((1 - way) * QUARTER, (2 - way) * QUARTER)
            gy_send[i, :, there] = total[:, there].astype(BF16)
            gy_send[i, :, here] = (total[:, here] + gr_recv[way, k].astype(F32)).astype(BF16)
            g_y(k, way).start()

        def own_head(k):
            g_acc[k] = pair_sum(3 * OWN_HEADS + k)

        steps = (
            opposite_head,
            functools.partial(next_head, 0),
            functools.partial(next_head, 1),
            own_head,
        )
        each(OWN_HEADS, steps[part])

    def arrive(i):
        @pl.when(i + AHEAD < HEADS)
        def _():
            start_kv(jnp.minimum(i + AHEAD, HEADS - 1))

        kv_far(i).wait_recv()
        kv_relay(i).start()

    def forward(i):
        kv_sib(i).wait_recv()
        kv_relay(i).wait_recv()
        scores = scores_of(i)
        top = jnp.max(scores, axis=1, keepdims=True)
        weights = jnp.exp2(scores - top)
        total = jnp.sum(weights, axis=1, keepdims=True)
        lse_s[i] = top + jnp.log2(total)
        probs = (weights * (1.0 / total)).astype(BF16)
        values = kv[i, :, :, DIM:].reshape(4 * TOK, DIM)
        attended = mm(probs, values, NN).astype(BF16)
        o_s[:, o_columns(i)] = attended
        g_send[i] = mm(attended, gp[0, :, other], TN).astype(BF16)
        g_pair(i).start()
        g_own[i] = mm(attended, gp[0, :, mine], TN)

    def far_send(i):
        d_pair(i).wait_recv()
        d_x[i] = (d_rs[i % 2] + d_sib_r[i, 1].astype(F32)).astype(BF16)
        d_far(i).start()

    def backward(b):
        i = back_order(b)

        @pl.when(b >= 1)
        def _():
            far_send(jnp.maximum(b - 1, 0))

        h = head(i)
        w_head = w_all[pl.ds(pl.multiple_of(h * DIM, DIM), DIM), :]
        grad_att = mm(gp[0], w_head, NT).astype(BF16)
        delta = jnp.sum(grad_att.astype(F32) * o_s[:, o_columns(i)].astype(F32), axis=1, keepdims=True)
        probs = jnp.exp2(scores_of(i) - lse_s[i])
        values = kv[i, :, :, DIM:].reshape(4 * TOK, DIM)
        dprobs = mm(grad_att, values, NT)
        dscores = (probs * (dprobs - delta)).astype(BF16)
        probs_b = probs.astype(BF16)
        keys = kv[i, :, :, 0:DIM].reshape(4 * TOK, DIM)
        grad_o[0, h, :, 0:DIM] = (mm(dscores, keys, NN) * SCALE).astype(BF16)
        dk = mm(dscores, q_s[h], TN) * SCALE
        dv = mm(probs_b, grad_att, TN)
        d_own[b, :, 0:DIM] = dk[0:TOK]
        d_own[b, :, DIM:] = dv[0:TOK]
        d_sib[b, 0, :, 0:DIM] = dk[TOK : 2 * TOK].astype(BF16)
        d_sib[b, 0, :, DIM:] = dv[TOK : 2 * TOK].astype(BF16)
        d_sib[b, 1, :, 0:DIM] = dk[3 * TOK :].astype(BF16)
        d_sib[b, 1, :, DIM:] = dv[3 * TOK :].astype(BF16)
        d_pair(b).start()
        d_rs[b % 2, :, 0:DIM] = dk[2 * TOK : 3 * TOK]
        d_rs[b % 2, :, DIM:] = dv[2 * TOK : 3 * TOK]

    def pass_slab(n):
        d = z_order(n)
        z_wait(d).wait_recv()
        y_copy(d, 0).start()
        y_copy(d, 1).start()

    def relay_slab(d):
        y_wait(d, 0).wait_recv()
        y_wait(d, 1).wait_recv()
        y_relay(d).start()

    def weight_step(t):
        for n in WEIGHT_SEND.get(t, ()):
            z_copy(z_order(n)).start()
        for n in WEIGHT_PASS.get(t, ()):
            pass_slab(n)
        for n in WEIGHT_RELAY.get(t, ()):
            relay_slab(0 if n == 0 else z_order(n - 1))
        if t == WEIGHT_OWN:
            block_copy(0).start()
        if t == WEIGHT_NEAR:
            block_copy(1).start()
            block_copy(2).start()
        if t == WEIGHT_LAST:
            for d in range(NZ):
                y_relay_wait(d).wait_recv()
            block_copy(3).start()

    def own_sum():
        g_stage(3)
        for k in range(OWN_HEADS):
            g_y(k, 0).wait_recv()
            g_y(k, 1).wait_recv()
            total = g_acc[k] + gy_recv[0, k].astype(F32) + gy_recv[1, k].astype(F32)
            g_acc[k] = total
            gz_send[k * DIM : (k + 1) * DIM] = total.astype(BF16)

    def step(t):
        @pl.when(t < HEADS)
        def _():
            i = jnp.minimum(t, HEADS - 1)
            arrive(i)

        for at in range(WEIGHT_LAST + 1):

            @pl.when(t == at)
            def _(at=at):
                weight_step(at)

        for part, at in enumerate(G_AT):

            @pl.when(t == at)
            def _(part=part):
                g_stage(part)

        @pl.when(t == GZ_AT)
        def _():
            own_sum()

        for part in range(4):

            @pl.when(t == GZ_AT + part)
            def _(part=part):
                for n in (2 * part, 2 * part + 1)[: NZ - 1 - 2 * part]:
                    g_z(z_order(n)).start()

        for k in range(4):

            @pl.when(t == LAG + OWN_HEADS * k)
            def _(k=k):
                block_wait(k).wait_recv()

        @pl.when(t < HEADS)
        def _():
            forward(jnp.minimum(t, HEADS - 1))

        @pl.when(t >= LAG)
        def _():
            backward(jnp.maximum(t - LAG, 0))

    each(HEADS + LAG, step)
    far_send(HEADS - 1)

    def project(k):
        columns = pl.ds(pl.multiple_of(k * TOK, TOK), TOK)
        proj_o[0, :, columns] = mm(o_s[...], w_all[:, columns], NN).astype(BF16)

    each(WIDTH // TOK, project)

    def finish(i):
        d_far(i).wait_recv()
        total = d_own[i] + d_sib_r[i, 0].astype(F32) + d_x_r[i].astype(F32)
        grad_o[0, head(back_order(i)), :, DIM:] = total.astype(BF16)

    each(3, finish)

    for d in range(1, NZ):
        g_z(d).wait_recv()
    acc = g_acc.reshape(BLOCK, HALF)
    total = acc[pl.ds(pl.multiple_of(SLAB * z, 8), SLAB)]
    for d in range(1, NZ):
        total = total + gz_recv[d - 1].astype(F32)
    gx_in[...] = total
    for k in range(NX):
        gx_send[k] = jnp.zeros_like(gx_send[k])
        gx_send[k, 0:CHIP_ROWS] = gx_in[k * CHIP_ROWS : (k + 1) * CHIP_ROWS]
    for d in range(1, NX):
        g_x(d).start()

    each(3, lambda i: finish(i + 3))

    for d in range(1, NX):
        g_x(d).wait_recv()
    total = gx_send[x]
    for d in range(1, NX):
        total = total + gx_recv[d - 1]
    for k in range(2):
        gc_send[k] = jnp.zeros_like(gc_send[k])
        gc_send[k, 0:DEV_ROWS] = total[k * DEV_ROWS : (k + 1) * DEV_ROWS]
    g_c.start()

    each(HEADS - 6, lambda i: finish(i + 6))

    g_c.wait_recv()
    gw_o[:, mine] = gc_send[c, 0:DEV_ROWS]
    gw_o[:, other] = gc_recv[0:DEV_ROWS]

    def sent(i):
        kv_far(i).wait_send()
        kv_sib(i).wait_send()
        kv_relay(i).wait_send()
        g_pair(i).wait_send()
        d_pair(i).wait_send()
        d_far(i).wait_send()

    each(HEADS, sent)

    def sent_g(k):
        for way in range(2):
            g_half(k, way).wait_send()
            g_y(k, way).wait_send()

    each(OWN_HEADS, sent_g)
    pair_copy.wait_send()
    g_c.wait_send()
    for d in range(1, NX):
        x_copy(d).wait_send()
        g_x(d).wait_send()
    for d in range(1, NZ):
        z_copy(d).wait_send()
        g_z(d).wait_send()

    def sent_y(d):
        y_copy(d, 0).wait_send()
        y_copy(d, 1).wait_send()
        y_relay(d).wait_send()

    each(NZ, sent_y)
    for k in range(4):
        block_copy(k).wait_send()


def hand_over(proj, grad, gw, proj_o, grad_o, gw_o, sems):
    copies = [pltpu.make_async_copy(gw, gw_o, sems.at[0])]
    for k in range(2):
        rows = pl.ds(k * (TOK // 2), TOK // 2)
        copies.append(pltpu.make_async_copy(proj.at[0, rows], proj_o.at[0, rows], sems.at[1 + k]))
    for h in range(HEADS):
        copies.append(pltpu.make_async_copy(grad.at[0, h], grad_o.at[0, h], sems.at[3 + h]))
    for copy in copies:
        copy.start()
    for copy in copies:
        copy.wait()


def local(qkv, out_weight, grad_projected, group_span, clip_length):
    vmem = functools.partial(pl.BlockSpec, memory_space=pltpu.VMEM)
    smem = functools.partial(pl.BlockSpec, memory_space=pltpu.SMEM)
    sem = pltpu.SemaphoreType.DMA
    scratch = [
        pltpu.VMEM((HEADS, TOK, DIM), BF16),
        pltpu.VMEM((HEADS, 4, TOK, 2 * DIM), BF16),
        pltpu.VMEM((8, 4 * TOK), F32),
        pltpu.VMEM((WIDTH, WIDTH), BF16),
        pltpu.VMEM((TOK, WIDTH), BF16),
        pltpu.VMEM((HEADS, TOK, 1), F32),
        pltpu.VMEM((8, HALF), F32),
        pltpu.VMEM((2, 8, HALF), F32),
        pltpu.VMEM((16, HALF), F32),
        pltpu.VMEM((NX, 16, HALF), BF16),
        pltpu.VMEM((SLAB, HALF), F32),
        pltpu.VMEM((HEADS, DIM, HALF), F32),
        pltpu.VMEM((OWN_HEADS, DIM, HALF), F32),
        pltpu.VMEM((HEADS, DIM, HALF), BF16),
        pltpu.VMEM((HEADS, DIM, HALF), BF16),
        pltpu.VMEM((HEADS - OWN_HEADS, DIM, HALF), BF16),
        pltpu.VMEM((2, OWN_HEADS, DIM, QUARTER), BF16),
        pltpu.VMEM((2, OWN_HEADS, DIM, HALF), BF16),
        pltpu.VMEM((BLOCK, HALF), BF16),
        pltpu.VMEM((NZ - 1, SLAB, HALF), BF16),
        pltpu.VMEM((SLAB, HALF), F32),
        pltpu.VMEM((NX, 16, HALF), F32),
        pltpu.VMEM((NX - 1, 16, HALF), F32),
        pltpu.VMEM((2, 8, HALF), F32),
        pltpu.VMEM((8, HALF), F32),
        pltpu.VMEM((HEADS, TOK, 2 * DIM), F32),
        pltpu.VMEM((2, TOK, 2 * DIM), F32),
        pltpu.VMEM((HEADS, 2, TOK, 2 * DIM), BF16),
        pltpu.VMEM((HEADS, 2, TOK, 2 * DIM), BF16),
        pltpu.VMEM((HEADS, TOK, 2 * DIM), BF16),
        pltpu.VMEM((HEADS, TOK, 2 * DIM), BF16),
        sem((1 + HEADS,)),
        sem((HEADS,)), sem((HEADS,)),
        sem((HEADS,)), sem((HEADS,)),
        sem((HEADS,)), sem((HEADS,)),
        sem, sem,
        sem((NX - 1,)), sem((NX - 1,)),
        sem((NZ - 1,)), sem((NZ - 1,)),
        sem((NZ, 2)), sem((NZ, 2)),
        sem((NZ,)), sem((NZ,)),
        sem((4,)), sem((4,)),
        sem((HEADS,)), sem((HEADS,)),
        sem((OWN_HEADS, 2)), sem((OWN_HEADS, 2)),
        sem((OWN_HEADS, 2)), sem((OWN_HEADS, 2)),
        sem((NZ - 1,)), sem((NZ - 1,)),
        sem((NX - 1,)), sem((NX - 1,)),
        sem, sem,
        sem((HEADS,)), sem((HEADS,)),
        sem((HEADS,)), sem((HEADS,)),
    ]
    results = pl.pallas_call(
        kernel,
        out_shape=(
            jax.ShapeDtypeStruct((1, TOK, WIDTH), BF16),
            jax.ShapeDtypeStruct((1, HEADS, TOK, 3 * DIM), BF16),
            jax.ShapeDtypeStruct((DEV_ROWS, WIDTH), F32),
        ),
        in_specs=[pl.BlockSpec(memory_space=pl.ANY), vmem(), vmem(), smem(), smem()],
        out_specs=(vmem(), vmem(), vmem()),
        scratch_shapes=scratch,
        compiler_params=pltpu.CompilerParams(
            collective_id=0, has_side_effects=True, vmem_limit_bytes=60 * 1024 * 1024
        ),
        cost_estimate=pl.CostEstimate(flops=10**10, bytes_accessed=10**7, transcendentals=7 * 10**6),
    )(qkv, out_weight, grad_projected, group_span, clip_length)
    hbm = functools.partial(pl.BlockSpec, memory_space=pl.ANY)
    return pl.pallas_call(
        hand_over,
        out_shape=tuple(jax.ShapeDtypeStruct(r.shape, r.dtype) for r in results),
        in_specs=[vmem(), vmem(), vmem()],
        out_specs=(hbm(), hbm(), hbm()),
        scratch_shapes=[sem((HEADS + 3,))],
    )(*results)


def solution(mesh):
    in_specs = (
        P("dp", None, "seq", None),
        P(("dp", "seq"), None),
        P("dp", "seq", None),
        P("dp", None),
        P("dp", None),
    )
    out_specs = (P("dp", "seq", None), P("dp", None, "seq", None), P(("dp", "seq"), None))
    return jax.shard_map(local, mesh=mesh, in_specs=in_specs, out_specs=out_specs, check_vma=False)
```

```python
import functools

import jax
import jax.numpy as jnp
from jax import lax
from jax.experimental import pallas as pl
from jax.experimental.pallas import tpu as pltpu
from jax.sharding import PartitionSpec as P

HEADS = 12
DIM = 128
TOK = 256
WIDTH = 1536
HALF = WIDTH // 2
QUARTER = HALF // 2
NY = 4
NZ = 8
NX = 4
SLAB = 48
BLOCK = SLAB * NZ
OWN_HEADS = HEADS // NY
CHIP_ROWS = 12
DEV_ROWS = 6
AHEAD = 2
LAG = 9
WEIGHT_SEND = {0: (2, 3), 1: (4, 5), 2: (6,)}
WEIGHT_PASS = {2: (0, 1), 3: (2, 3), 4: (4, 5), 5: (6,)}
WEIGHT_RELAY = {2: (0,), 4: (1, 2), 5: (3, 4), 6: (5, 6), 7: (7,)}
WEIGHT_OWN, WEIGHT_NEAR, WEIGHT_LAST = 6, 8, 13
G_AT = (8, 10, 11)
GZ_AT = 16
FLOOR = -1e30
SCALE = DIM**-0.5
LOG2E = 1.4426950408889634
MESH = pl.DeviceIdType.MESH
F32 = jnp.float32
BF16 = jnp.bfloat16


def mm(a, b, dims):
    return lax.dot_general(a, b, (dims, ((), ())), preferred_element_type=F32)


NN = ((1,), (0,))
NT = ((1,), (1,))
TN = ((0,), (0,))


def kernel(
    qkv, w_own, gp, span, clip,
    proj_o, grad_o, gw_o,
    q_s, kv, bias_s, w_all, o_s, lse_s,
    w_send, w_pair, w_tmp, w_x, w_slab,
    g_own, g_acc, g_send, g_recv, gy_send, gr_recv, gy_recv, gz_send, gz_recv,
    gx_in, gx_send, gx_recv, gc_send, gc_recv,
    d_own, d_rs, d_sib, d_sib_r, d_x, d_x_r,
    loc_sem, ks_s, ks_r, kx_s, kx_r, kf_s, kf_r,
    wa_s, wa_r, wx_s, wx_r, wz_s, wz_r, wy_s, wy_r, wf_s, wf_r, wb_s, wb_r,
    gs_s, gs_r, gr_s, gr_r, gy_s, gy_r, gz_s, gz_r, gx_s, gx_r, gc_s, gc_r,
    ds_s, ds_r, dx_s, dx_r,
):
    me = lax.axis_index("seq")
    y = lax.axis_index("dp")
    c = me % 2
    x = (me // 2) % NX
    z = me // (2 * NX)
    sib = me + 1 - 2 * c
    far = me + 2 - 4 * (x % 2)
    cross = far + 1 - 2 * c

    def at_x(xx):
        return {"seq": (z * NX + xx) * 2 + c}

    def at_z(zz):
        return {"seq": (zz * NX + x) * 2 + c}

    def at_y(yy):
        return {"dp": yy}

    at_sib = {"seq": sib}
    at_far = {"seq": far}

    def rdma(src, dst, send, recv, device):
        return pltpu.make_async_remote_copy(
            src_ref=src, dst_ref=dst, send_sem=send, recv_sem=recv,
            device_id=device, device_id_type=MESH,
        )

    partners = [at_sib]
    partners += [at_x((x + d) % NX) for d in range(1, NX)]
    partners += [at_z((z + d) % NZ) for d in range(1, NZ)]
    partners += [at_y((y + 1) % NY), at_y((y + NY - 1) % NY)]
    barrier = pltpu.get_barrier_semaphore()
    for partner in partners:
        pl.semaphore_signal(barrier, inc=1, device_id=partner, device_id_type=MESH)
    pl.semaphore_wait(barrier, len(partners))

    def head(i):
        part = i // OWN_HEADS
        owner = y + jnp.where(part == 0, 2, jnp.where(part == 1, 1, jnp.where(part == 2, 3, 0)))
        return (OWN_HEADS * owner + i % OWN_HEADS) % HEADS

    def back_order(b):
        return OWN_HEADS * (NY - 1 - b // OWN_HEADS) + b % OWN_HEADS

    def kv_sib(i):
        return rdma(qkv.at[0, head(i), :, pl.ds(DIM, 2 * DIM)], kv.at[i, 1], ks_s.at[i], ks_r.at[i], at_sib)

    def kv_far(i):
        return rdma(qkv.at[0, head(i), :, pl.ds(DIM, 2 * DIM)], kv.at[i, 2], kx_s.at[i], kx_r.at[i], at_far)

    def kv_relay(i):
        return rdma(kv.at[i, 2], kv.at[i, 3], kf_s.at[i], kf_r.at[i], at_sib)

    def kv_own(i):
        return pltpu.make_async_copy(qkv.at[0, head(i), :, pl.ds(DIM, 2 * DIM)], kv.at[i, 0], loc_sem.at[1 + i])

    q_copy = pltpu.make_async_copy(qkv.at[0, :, :, pl.ds(0, DIM)], q_s, loc_sem.at[0])

    mine = pl.ds(pl.multiple_of(c * HALF, HALF), HALF)
    other = pl.ds(pl.multiple_of((1 - c) * HALF, HALF), HALF)

    def slab(yy, zz):
        return w_all.at[pl.ds(pl.multiple_of(SLAB * (NZ * yy + zz), 16), SLAB), mine]

    pair_copy = rdma(w_send, w_pair.at[c], wa_s, wa_r, at_sib)
    pair_wait = rdma(w_send, w_pair.at[1 - c], wa_s, wa_r, at_sib)

    def x_copy(d):
        return rdma(w_x.at[x], w_x.at[x], wx_s.at[d - 1], wx_r.at[d - 1], at_x((x + d) % NX))

    def x_wait(d):
        back = (x + NX - d) % NX
        return rdma(w_x.at[back], w_x.at[back], wx_s.at[d - 1], wx_r.at[d - 1], at_x(back))

    def z_copy(d):
        return rdma(slab(y, z), slab(y, z), wz_s.at[d - 1], wz_r.at[d - 1], at_z((z + d) % NZ))

    def z_wait(d):
        back = (z + NZ - d) % NZ
        return rdma(slab(y, back), slab(y, back), wz_s.at[d - 1], wz_r.at[d - 1], at_z(back))

    up, down = (y + 1) % NY, (y + NY - 1) % NY
    opposite = (y + 2) % NY

    def y_copy(d, way):
        zz = (z + NZ - d) % NZ
        return rdma(slab(y, zz), slab(y, zz), wy_s.at[d, way], wy_r.at[d, way], at_y(up if way == 0 else down))

    def y_wait(d, way):
        zz = (z + NZ - d) % NZ
        yy = down if way == 0 else up
        return rdma(slab(yy, zz), slab(yy, zz), wy_s.at[d, way], wy_r.at[d, way], at_y(yy))

    def y_relay(d):
        zz = (z + NZ - d) % NZ
        odd = d % 2
        yy = (y + NY - 1 + 2 * odd) % NY
        to = (y + 1 + 2 * odd) % NY
        return rdma(slab(yy, zz), slab(yy, zz), wf_s.at[d], wf_r.at[d], at_y(to))

    def y_relay_wait(d):
        zz = (z + NZ - d) % NZ
        return rdma(slab(opposite, zz), slab(opposite, zz), wf_s.at[d], wf_r.at[d], at_y(up))

    def rows_block(yy, columns):
        return w_all.at[pl.ds(pl.multiple_of(BLOCK * yy, 16), BLOCK), columns]

    def block_copy(k):
        yy = (y, down, up, opposite)[k]
        return rdma(rows_block(yy, mine), rows_block(yy, mine), wb_s.at[k], wb_r.at[k], at_sib)

    def block_wait(k):
        yy = (y, down, up, opposite)[k]
        return rdma(rows_block(yy, other), rows_block(yy, other), wb_s.at[k], wb_r.at[k], at_sib)

    def z_order(i):
        return 1 + i // 2 + (i % 2) * (NZ - 2 - 2 * (i // 2))

    def g_pair(i):
        return rdma(g_send.at[i], g_recv.at[i], gs_s.at[i], gs_r.at[i], at_sib)

    def g_half(k, way):
        columns = pl.ds(way * QUARTER, QUARTER)
        to = at_y(up if way == 0 else down)
        return rdma(gy_send.at[k, :, columns], gr_recv.at[way, k], gr_s.at[k, way], gr_r.at[k, way], to)

    def g_y(k, way):
        to = at_y(up if way == 0 else down)
        return rdma(gy_send.at[OWN_HEADS * (1 + way) + k], gy_recv.at[way, k], gy_s.at[k, way], gy_r.at[k, way], to)

    def g_z(d):
        zz = (z + d) % NZ
        rows = gz_send.at[pl.ds(pl.multiple_of(SLAB * zz, 16), SLAB)]
        return rdma(rows, gz_recv.at[d - 1], gz_s.at[d - 1], gz_r.at[d - 1], at_z(zz))

    def g_x(d):
        xx = (x + d) % NX
        return rdma(gx_send.at[xx], gx_recv.at[d - 1], gx_s.at[d - 1], gx_r.at[d - 1], at_x(xx))

    g_c = rdma(gc_send.at[1 - c], gc_recv, gc_s, gc_r, at_sib)

    def d_pair(i):
        return rdma(d_sib.at[i], d_sib_r.at[i], ds_s.at[i], ds_r.at[i], at_sib)

    def d_far(i):
        return rdma(d_x.at[i], d_x_r.at[i], dx_s.at[i], dx_r.at[i], at_far)

    def each(count, step):
        def body(i, carry):
            step(i)
            return carry

        lax.fori_loop(0, count, body, 0)

    w_send[...] = jnp.zeros_like(w_send)
    w_send[0:DEV_ROWS] = w_own[:, other].astype(F32)
    pair_copy.start()

    def start_kv(i):
        kv_far(i).start()
        kv_sib(i).start()

    start_kv(0)
    q_copy.start()
    each(HEADS, lambda i: kv_own(i).start())

    def base_of(s):
        g = span[0, s]
        return s - jnp.where(g == 1, 0, jnp.where(g == 2, s % 2, s % 4))

    my_base = base_of(me)
    place = lax.broadcasted_iota(jnp.int32, (8, TOK), 1)
    for r, s in enumerate((me, sib, far, cross)):
        base = base_of(s)
        live = jnp.where(base == my_base, clip[0, s] - (s - base) * TOK, 0)
        bias_s[:, r * TOK : (r + 1) * TOK] = jnp.where(place < live, 0.0, FLOOR)

    pair_wait.wait_recv()
    w_tmp[...] = jnp.zeros_like(w_tmp)
    own_rows = w_own[:, mine].astype(F32)
    their_rows = jnp.where(c == 0, w_pair[1, 0:DEV_ROWS], w_pair[0, 0:DEV_ROWS])
    w_tmp[0:DEV_ROWS] = jnp.where(c == 0, own_rows, their_rows)
    w_tmp[DEV_ROWS:CHIP_ROWS] = jnp.where(c == 0, their_rows, own_rows)
    w_x[x] = w_tmp[...].astype(BF16)
    for d in range(1, NX):
        x_copy(d).start()
    start_kv(1)
    for d in range(1, NX):
        x_wait(d).wait_recv()
    for k in range(NX):
        w_slab[k * CHIP_ROWS : (k + 1) * CHIP_ROWS] = w_x[k].astype(F32)[0:CHIP_ROWS]
    slab(y, z)[...] = w_slab[...].astype(BF16)
    for i in range(2):
        z_copy(z_order(i)).start()
    y_copy(0, 0).start()
    y_copy(0, 1).start()

    q_copy.wait()
    each(HEADS, lambda i: kv_own(i).wait())

    def scores_of(i):
        keys = kv[i, :, :, 0:DIM].reshape(4 * TOK, DIM)
        raw = mm(q_s[head(i)], keys, NT)
        return raw * (SCALE * LOG2E) + bias_s[0:1, :]

    def o_columns(i):
        return pl.ds(pl.multiple_of(head(i) * DIM, DIM), DIM)

    def pair_sum(i):
        g_pair(i).wait_recv()
        return g_own[i] + g_recv[i].astype(F32)

    def g_stage(part):
        def opposite_head(k):
            gy_send[k] = pair_sum(k).astype(BF16)
            g_half(k, 0).start()
            g_half(k, 1).start()

        def next_head(way, k):
            i = OWN_HEADS * (1 + way) + k
            total = pair_sum(i)
            g_half(k, way).wait_recv()
            here = slice(way * QUARTER, (way + 1) * QUARTER)
            there = slice((1 - way) * QUARTER, (2 - way) * QUARTER)
            gy_send[i, :, there] = total[:, there].astype(BF16)
            gy_send[i, :, here] = (total[:, here] + gr_recv[way, k].astype(F32)).astype(BF16)
            g_y(k, way).start()

        def own_head(k):
            g_acc[k] = pair_sum(3 * OWN_HEADS + k)

        steps = (
            opposite_head,
            functools.partial(next_head, 0),
            functools.partial(next_head, 1),
            own_head,
        )
        each(OWN_HEADS, steps[part])

    def arrive(i):
        @pl.when(i + AHEAD < HEADS)
        def _():
            start_kv(jnp.minimum(i + AHEAD, HEADS - 1))

        kv_far(i).wait_recv()
        kv_relay(i).start()

    def forward(i):
        kv_sib(i).wait_recv()
        kv_relay(i).wait_recv()
        scores = scores_of(i)
        top = jnp.max(scores, axis=1, keepdims=True)
        weights = jnp.exp2(scores - top)
        total = jnp.sum(weights, axis=1, keepdims=True)
        lse_s[i] = top + jnp.log2(total)
        probs = (weights * (1.0 / total)).astype(BF16)
        values = kv[i, :, :, DIM:].reshape(4 * TOK, DIM)
        attended = mm(probs, values, NN).astype(BF16)
        o_s[:, o_columns(i)] = attended
        g_send[i] = mm(attended, gp[0, :, other], TN).astype(BF16)
        g_pair(i).start()
        g_own[i] = mm(attended, gp[0, :, mine], TN)

    def far_send(i):
        d_pair(i).wait_recv()
        d_x[i] = (d_rs[i % 2] + d_sib_r[i, 1].astype(F32)).astype(BF16)
        d_far(i).start()

    def backward(b):
        i = back_order(b)

        @pl.when(b >= 1)
        def _():
            far_send(jnp.maximum(b - 1, 0))

        h = head(i)
        w_head = w_all[pl.ds(pl.multiple_of(h * DIM, DIM), DIM), :]
        grad_att = mm(gp[0], w_head, NT).astype(BF16)
        delta = jnp.sum(grad_att.astype(F32) * o_s[:, o_columns(i)].astype(F32), axis=1, keepdims=True)
        probs = jnp.exp2(scores_of(i) - lse_s[i])
        values = kv[i, :, :, DIM:].reshape(4 * TOK, DIM)
        dprobs = mm(grad_att, values, NT)
        dscores = (probs * (dprobs - delta)).astype(BF16)
        probs_b = probs.astype(BF16)
        keys = kv[i, :, :, 0:DIM].reshape(4 * TOK, DIM)
        grad_o[0, h, :, 0:DIM] = (mm(dscores, keys, NN) * SCALE).astype(BF16)
        dk = mm(dscores, q_s[h], TN) * SCALE
        dv = mm(probs_b, grad_att, TN)
        d_own[b, :, 0:DIM] = dk[0:TOK]
        d_own[b, :, DIM:] = dv[0:TOK]
        d_sib[b, 0, :, 0:DIM] = dk[TOK : 2 * TOK].astype(BF16)
        d_sib[b, 0, :, DIM:] = dv[TOK : 2 * TOK].astype(BF16)
        d_sib[b, 1, :, 0:DIM] = dk[3 * TOK :].astype(BF16)
        d_sib[b, 1, :, DIM:] = dv[3 * TOK :].astype(BF16)
        d_pair(b).start()
        d_rs[b % 2, :, 0:DIM] = dk[2 * TOK : 3 * TOK]
        d_rs[b % 2, :, DIM:] = dv[2 * TOK : 3 * TOK]

    def pass_slab(n):
        d = z_order(n)
        z_wait(d).wait_recv()
        y_copy(d, 0).start()
        y_copy(d, 1).start()

    def relay_slab(d):
        y_wait(d, 0).wait_recv()
        y_wait(d, 1).wait_recv()
        y_relay(d).start()

    def weight_step(t):
        for n in WEIGHT_SEND.get(t, ()):
            z_copy(z_order(n)).start()
        for n in WEIGHT_PASS.get(t, ()):
            pass_slab(n)
        for n in WEIGHT_RELAY.get(t, ()):
            relay_slab(0 if n == 0 else z_order(n - 1))
        if t == WEIGHT_OWN:
            block_copy(0).start()
        if t == WEIGHT_NEAR:
            block_copy(1).start()
            block_copy(2).start()
        if t == WEIGHT_LAST:
            for d in range(NZ):
                y_relay_wait(d).wait_recv()
            block_copy(3).start()

    def own_sum():
        g_stage(3)
        for k in range(OWN_HEADS):
            g_y(k, 0).wait_recv()
            g_y(k, 1).wait_recv()
            total = g_acc[k] + gy_recv[0, k].astype(F32) + gy_recv[1, k].astype(F32)
            g_acc[k] = total
            gz_send[k * DIM : (k + 1) * DIM] = total.astype(BF16)

    def step(t):
        @pl.when(t < HEADS)
        def _():
            i = jnp.minimum(t, HEADS - 1)
            arrive(i)

        for at in range(WEIGHT_LAST + 1):

            @pl.when(t == at)
            def _(at=at):
                weight_step(at)

        for part, at in enumerate(G_AT):

            @pl.when(t == at)
            def _(part=part):
                g_stage(part)

        @pl.when(t == GZ_AT)
        def _():
            own_sum()

        for part in range(4):

            @pl.when(t == GZ_AT + part)
            def _(part=part):
                for n in (2 * part, 2 * part + 1)[: NZ - 1 - 2 * part]:
                    g_z(z_order(n)).start()

        for k in range(4):

            @pl.when(t == LAG + OWN_HEADS * k)
            def _(k=k):
                block_wait(k).wait_recv()

        @pl.when(t < HEADS)
        def _():
            forward(jnp.minimum(t, HEADS - 1))

        @pl.when(t >= LAG)
        def _():
            backward(jnp.maximum(t - LAG, 0))

    each(HEADS + LAG, step)
    far_send(HEADS - 1)

    def project(k):
        columns = pl.ds(pl.multiple_of(k * TOK, TOK), TOK)
        proj_o[0, :, columns] = mm(o_s[...], w_all[:, columns], NN).astype(BF16)

    each(WIDTH // TOK, project)

    def finish(i):
        d_far(i).wait_recv()
        total = d_own[i] + d_sib_r[i, 0].astype(F32) + d_x_r[i].astype(F32)
        grad_o[0, head(back_order(i)), :, DIM:] = total.astype(BF16)

    each(3, finish)

    for d in range(1, NZ):
        g_z(d).wait_recv()
    acc = g_acc.reshape(BLOCK, HALF)
    total = acc[pl.ds(pl.multiple_of(SLAB * z, 8), SLAB)]
    for d in range(1, NZ):
        total = total + gz_recv[d - 1].astype(F32)
    gx_in[...] = total
    for k in range(NX):
        gx_send[k] = jnp.zeros_like(gx_send[k])
        gx_send[k, 0:CHIP_ROWS] = gx_in[k * CHIP_ROWS : (k + 1) * CHIP_ROWS]
    for d in range(1, NX):
        g_x(d).start()

    each(3, lambda i: finish(i + 3))

    for d in range(1, NX):
        g_x(d).wait_recv()
    total = gx_send[x]
    for d in range(1, NX):
        total = total + gx_recv[d - 1]
    for k in range(2):
        gc_send[k] = jnp.zeros_like(gc_send[k])
        gc_send[k, 0:DEV_ROWS] = total[k * DEV_ROWS : (k + 1) * DEV_ROWS]
    g_c.start()

    each(HEADS - 6, lambda i: finish(i + 6))

    g_c.wait_recv()
    gw_o[:, mine] = gc_send[c, 0:DEV_ROWS]
    gw_o[:, other] = gc_recv[0:DEV_ROWS]

    def sent(i):
        kv_far(i).wait_send()
        kv_sib(i).wait_send()
        kv_relay(i).wait_send()
        g_pair(i).wait_send()
        d_pair(i).wait_send()
        d_far(i).wait_send()

    each(HEADS, sent)

    def sent_g(k):
        for way in range(2):
            g_half(k, way).wait_send()
            g_y(k, way).wait_send()

    each(OWN_HEADS, sent_g)
    pair_copy.wait_send()
    g_c.wait_send()
    for d in range(1, NX):
        x_copy(d).wait_send()
        g_x(d).wait_send()
    for d in range(1, NZ):
        z_copy(d).wait_send()
        g_z(d).wait_send()

    def sent_y(d):
        y_copy(d, 0).wait_send()
        y_copy(d, 1).wait_send()
        y_relay(d).wait_send()

    each(NZ, sent_y)
    for k in range(4):
        block_copy(k).wait_send()


def hand_over(proj, grad, gw, proj_o, grad_o, gw_o, sems):
    copies = [pltpu.make_async_copy(gw, gw_o, sems.at[0])]
    for k in range(2):
        rows = pl.ds(k * (TOK // 2), TOK // 2)
        copies.append(pltpu.make_async_copy(proj.at[0, rows], proj_o.at[0, rows], sems.at[1 + k]))
    for h in range(HEADS):
        copies.append(pltpu.make_async_copy(grad.at[0, h], grad_o.at[0, h], sems.at[3 + h]))
    for copy in copies:
        copy.start()
    for copy in copies:
        copy.wait()


def local(qkv, out_weight, grad_projected, group_span, clip_length):
    vmem = functools.partial(pl.BlockSpec, memory_space=pltpu.VMEM)
    smem = functools.partial(pl.BlockSpec, memory_space=pltpu.SMEM)
    sem = pltpu.SemaphoreType.DMA
    scratch = [
        pltpu.VMEM((HEADS, TOK, DIM), BF16),
        pltpu.VMEM((HEADS, 4, TOK, 2 * DIM), BF16),
        pltpu.VMEM((8, 4 * TOK), F32),
        pltpu.VMEM((WIDTH, WIDTH), BF16),
        pltpu.VMEM((TOK, WIDTH), BF16),
        pltpu.VMEM((HEADS, TOK, 1), F32),
        pltpu.VMEM((8, HALF), F32),
        pltpu.VMEM((2, 8, HALF), F32),
        pltpu.VMEM((16, HALF), F32),
        pltpu.VMEM((NX, 16, HALF), BF16),
        pltpu.VMEM((SLAB, HALF), F32),
        pltpu.VMEM((HEADS, DIM, HALF), F32),
        pltpu.VMEM((OWN_HEADS, DIM, HALF), F32),
        pltpu.VMEM((HEADS, DIM, HALF), BF16),
        pltpu.VMEM((HEADS, DIM, HALF), BF16),
        pltpu.VMEM((HEADS - OWN_HEADS, DIM, HALF), BF16),
        pltpu.VMEM((2, OWN_HEADS, DIM, QUARTER), BF16),
        pltpu.VMEM((2, OWN_HEADS, DIM, HALF), BF16),
        pltpu.VMEM((BLOCK, HALF), BF16),
        pltpu.VMEM((NZ - 1, SLAB, HALF), BF16),
        pltpu.VMEM((SLAB, HALF), F32),
        pltpu.VMEM((NX, 16, HALF), F32),
        pltpu.VMEM((NX - 1, 16, HALF), F32),
        pltpu.VMEM((2, 8, HALF), F32),
        pltpu.VMEM((8, HALF), F32),
        pltpu.VMEM((HEADS, TOK, 2 * DIM), F32),
        pltpu.VMEM((2, TOK, 2 * DIM), F32),
        pltpu.VMEM((HEADS, 2, TOK, 2 * DIM), BF16),
        pltpu.VMEM((HEADS, 2, TOK, 2 * DIM), BF16),
        pltpu.VMEM((HEADS, TOK, 2 * DIM), BF16),
        pltpu.VMEM((HEADS, TOK, 2 * DIM), BF16),
        sem((1 + HEADS,)),
        sem((HEADS,)), sem((HEADS,)),
        sem((HEADS,)), sem((HEADS,)),
        sem((HEADS,)), sem((HEADS,)),
        sem, sem,
        sem((NX - 1,)), sem((NX - 1,)),
        sem((NZ - 1,)), sem((NZ - 1,)),
        sem((NZ, 2)), sem((NZ, 2)),
        sem((NZ,)), sem((NZ,)),
        sem((4,)), sem((4,)),
        sem((HEADS,)), sem((HEADS,)),
        sem((OWN_HEADS, 2)), sem((OWN_HEADS, 2)),
        sem((OWN_HEADS, 2)), sem((OWN_HEADS, 2)),
        sem((NZ - 1,)), sem((NZ - 1,)),
        sem((NX - 1,)), sem((NX - 1,)),
        sem, sem,
        sem((HEADS,)), sem((HEADS,)),
        sem((HEADS,)), sem((HEADS,)),
    ]
    results = pl.pallas_call(
        kernel,
        out_shape=(
            jax.ShapeDtypeStruct((1, TOK, WIDTH), BF16),
            jax.ShapeDtypeStruct((1, HEADS, TOK, 3 * DIM), BF16),
            jax.ShapeDtypeStruct((DEV_ROWS, WIDTH), F32),
        ),
        in_specs=[pl.BlockSpec(memory_space=pl.ANY), vmem(), vmem(), smem(), smem()],
        out_specs=(vmem(), vmem(), vmem()),
        scratch_shapes=scratch,
        compiler_params=pltpu.CompilerParams(
            collective_id=0, has_side_effects=True, vmem_limit_bytes=60 * 1024 * 1024
        ),
        cost_estimate=pl.CostEstimate(flops=10**10, bytes_accessed=10**7, transcendentals=7 * 10**6),
    )(qkv, out_weight, grad_projected, group_span, clip_length)
    hbm = functools.partial(pl.BlockSpec, memory_space=pl.ANY)
    return pl.pallas_call(
        hand_over,
        out_shape=tuple(jax.ShapeDtypeStruct(r.shape, r.dtype) for r in results),
        in_specs=[vmem(), vmem(), vmem()],
        out_specs=(hbm(), hbm(), hbm()),
        scratch_shapes=[sem((HEADS + 3,))],
    )(*results)


def solution(mesh):
    in_specs = (
        P("dp", None, "seq", None),
        P(("dp", "seq"), None),
        P("dp", "seq", None),
        P("dp", None),
        P("dp", None),
    )
    out_specs = (P("dp", "seq", None), P("dp", None, "seq", None), P(("dp", "seq"), None))
    return jax.shard_map(local, mesh=mesh, in_specs=in_specs, out_specs=out_specs, check_vma=False)
```

```python
import functools

import jax
import jax.numpy as jnp
from jax import lax
from jax.experimental import pallas as pl
from jax.experimental.pallas import tpu as pltpu
from jax.sharding import PartitionSpec as P

HEADS = 12
DIM = 128
TOK = 256
WIDTH = 1536
HALF = WIDTH // 2
QUARTER = HALF // 2
NY = 4
NZ = 8
NX = 4
SLAB = 48
BLOCK = SLAB * NZ
OWN_HEADS = HEADS // NY
CHIP_ROWS = 12
DEV_ROWS = 6
AHEAD = 2
LAG = 9
WEIGHT_SEND = {0: (2, 3), 1: (4, 5), 2: (6,)}
WEIGHT_PASS = {2: (0, 1), 3: (2, 3), 4: (4, 5), 5: (6,)}
WEIGHT_RELAY = {2: (0,), 4: (1, 2), 5: (3, 4), 6: (5, 6), 7: (7,)}
WEIGHT_OWN, WEIGHT_NEAR, WEIGHT_LAST = 6, 8, 13
G_AT = (7, 10, 11)
GZ_AT = 17
FLOOR = -1e30
SCALE = DIM**-0.5
LOG2E = 1.4426950408889634
MESH = pl.DeviceIdType.MESH
F32 = jnp.float32
BF16 = jnp.bfloat16


def mm(a, b, dims):
    return lax.dot_general(a, b, (dims, ((), ())), preferred_element_type=F32)


NN = ((1,), (0,))
NT = ((1,), (1,))
TN = ((0,), (0,))


def kernel(
    qkv, w_own, gp, span, clip,
    proj_o, grad_o, gw_o,
    q_s, kv, bias_s, w_all, o_s, lse_s,
    w_send, w_pair, w_tmp, w_x, w_slab,
    g_own, g_acc, g_send, g_recv, gy_send, gr_recv, gy_recv, gz_send, gz_recv,
    gx_in, gx_send, gx_recv, gc_send, gc_recv,
    d_own, d_rs, d_sib, d_sib_r, d_x, d_x_r,
    loc_sem, ks_s, ks_r, kx_s, kx_r, kf_s, kf_r,
    wa_s, wa_r, wx_s, wx_r, wz_s, wz_r, wy_s, wy_r, wf_s, wf_r, wb_s, wb_r,
    gs_s, gs_r, gr_s, gr_r, gy_s, gy_r, gz_s, gz_r, gx_s, gx_r, gc_s, gc_r,
    ds_s, ds_r, dx_s, dx_r,
):
    me = lax.axis_index("seq")
    y = lax.axis_index("dp")
    c = me % 2
    x = (me // 2) % NX
    z = me // (2 * NX)
    sib = me + 1 - 2 * c
    far = me + 2 - 4 * (x % 2)
    cross = far + 1 - 2 * c

    def at_x(xx):
        return {"seq": (z * NX + xx) * 2 + c}

    def at_z(zz):
        return {"seq": (zz * NX + x) * 2 + c}

    def at_y(yy):
        return {"dp": yy}

    at_sib = {"seq": sib}
    at_far = {"seq": far}

    def rdma(src, dst, send, recv, device):
        return pltpu.make_async_remote_copy(
            src_ref=src, dst_ref=dst, send_sem=send, recv_sem=recv,
            device_id=device, device_id_type=MESH,
        )

    partners = [at_sib]
    partners += [at_x((x + d) % NX) for d in range(1, NX)]
    partners += [at_z((z + d) % NZ) for d in range(1, NZ)]
    partners += [at_y((y + 1) % NY), at_y((y + NY - 1) % NY)]
    barrier = pltpu.get_barrier_semaphore()
    for partner in partners:
        pl.semaphore_signal(barrier, inc=1, device_id=partner, device_id_type=MESH)
    pl.semaphore_wait(barrier, len(partners))

    def head(i):
        part = i // OWN_HEADS
        owner = y + jnp.where(part == 0, 2, jnp.where(part == 1, 1, jnp.where(part == 2, 3, 0)))
        return (OWN_HEADS * owner + i % OWN_HEADS) % HEADS

    def back_order(b):
        return OWN_HEADS * (NY - 1 - b // OWN_HEADS) + b % OWN_HEADS

    def kv_sib(i):
        return rdma(qkv.at[0, head(i), :, pl.ds(DIM, 2 * DIM)], kv.at[i, 1], ks_s.at[i], ks_r.at[i], at_sib)

    def kv_far(i):
        return rdma(qkv.at[0, head(i), :, pl.ds(DIM, 2 * DIM)], kv.at[i, 2], kx_s.at[i], kx_r.at[i], at_far)

    def kv_relay(i):
        return rdma(kv.at[i, 2], kv.at[i, 3], kf_s.at[i], kf_r.at[i], at_sib)

    def kv_own(i):
        return pltpu.make_async_copy(qkv.at[0, head(i), :, pl.ds(DIM, 2 * DIM)], kv.at[i, 0], loc_sem.at[1 + i])

    q_copy = pltpu.make_async_copy(qkv.at[0, :, :, pl.ds(0, DIM)], q_s, loc_sem.at[0])

    mine = pl.ds(pl.multiple_of(c * HALF, HALF), HALF)
    other = pl.ds(pl.multiple_of((1 - c) * HALF, HALF), HALF)

    def slab(yy, zz):
        return w_all.at[pl.ds(pl.multiple_of(SLAB * (NZ * yy + zz), 16), SLAB), mine]

    pair_copy = rdma(w_send, w_pair.at[c], wa_s, wa_r, at_sib)
    pair_wait = rdma(w_send, w_pair.at[1 - c], wa_s, wa_r, at_sib)

    def x_copy(d):
        return rdma(w_x.at[x], w_x.at[x], wx_s.at[d - 1], wx_r.at[d - 1], at_x((x + d) % NX))

    def x_wait(d):
        back = (x + NX - d) % NX
        return rdma(w_x.at[back], w_x.at[back], wx_s.at[d - 1], wx_r.at[d - 1], at_x(back))

    def z_copy(d):
        return rdma(slab(y, z), slab(y, z), wz_s.at[d - 1], wz_r.at[d - 1], at_z((z + d) % NZ))

    def z_wait(d):
        back = (z + NZ - d) % NZ
        return rdma(slab(y, back), slab(y, back), wz_s.at[d - 1], wz_r.at[d - 1], at_z(back))

    up, down = (y + 1) % NY, (y + NY - 1) % NY
    opposite = (y + 2) % NY

    def y_copy(d, way):
        zz = (z + NZ - d) % NZ
        return rdma(slab(y, zz), slab(y, zz), wy_s.at[d, way], wy_r.at[d, way], at_y(up if way == 0 else down))

    def y_wait(d, way):
        zz = (z + NZ - d) % NZ
        yy = down if way == 0 else up
        return rdma(slab(yy, zz), slab(yy, zz), wy_s.at[d, way], wy_r.at[d, way], at_y(yy))

    def y_relay(d):
        zz = (z + NZ - d) % NZ
        odd = d % 2
        yy = (y + NY - 1 + 2 * odd) % NY
        to = (y + 1 + 2 * odd) % NY
        return rdma(slab(yy, zz), slab(yy, zz), wf_s.at[d], wf_r.at[d], at_y(to))

    def y_relay_wait(d):
        zz = (z + NZ - d) % NZ
        return rdma(slab(opposite, zz), slab(opposite, zz), wf_s.at[d], wf_r.at[d], at_y(up))

    def rows_block(yy, columns):
        return w_all.at[pl.ds(pl.multiple_of(BLOCK * yy, 16), BLOCK), columns]

    def block_copy(k):
        yy = (y, down, up, opposite)[k]
        return rdma(rows_block(yy, mine), rows_block(yy, mine), wb_s.at[k], wb_r.at[k], at_sib)

    def block_wait(k):
        yy = (y, down, up, opposite)[k]
        return rdma(rows_block(yy, other), rows_block(yy, other), wb_s.at[k], wb_r.at[k], at_sib)

    def z_order(i):
        return 1 + i // 2 + (i % 2) * (NZ - 2 - 2 * (i // 2))

    def g_pair(i):
        return rdma(g_send.at[i], g_recv.at[i], gs_s.at[i], gs_r.at[i], at_sib)

    def g_half(k, way):
        columns = pl.ds(way * QUARTER, QUARTER)
        to = at_y(up if way == 0 else down)
        return rdma(gy_send.at[k, :, columns], gr_recv.at[way, k], gr_s.at[k, way], gr_r.at[k, way], to)

    def g_y(k, way):
        to = at_y(up if way == 0 else down)
        return rdma(gy_send.at[OWN_HEADS * (1 + way) + k], gy_recv.at[way, k], gy_s.at[k, way], gy_r.at[k, way], to)

    def g_z(d):
        zz = (z + d) % NZ
        rows = gz_send.at[pl.ds(pl.multiple_of(SLAB * zz, 16), SLAB)]
        return rdma(rows, gz_recv.at[d - 1], gz_s.at[d - 1], gz_r.at[d - 1], at_z(zz))

    def g_x(d):
        xx = (x + d) % NX
        return rdma(gx_send.at[xx], gx_recv.at[d - 1], gx_s.at[d - 1], gx_r.at[d - 1], at_x(xx))

    g_c = rdma(gc_send.at[1 - c], gc_recv, gc_s, gc_r, at_sib)

    def d_pair(i):
        return rdma(d_sib.at[i], d_sib_r.at[i], ds_s.at[i], ds_r.at[i], at_sib)

    def d_far(i):
        return rdma(d_x.at[i], d_x_r.at[i], dx_s.at[i], dx_r.at[i], at_far)

    def each(count, step):
        def body(i, carry):
            step(i)
            return carry

        lax.fori_loop(0, count, body, 0)

    w_send[...] = jnp.zeros_like(w_send)
    w_send[0:DEV_ROWS] = w_own[:, other].astype(F32)
    pair_copy.start()

    def start_kv(i):
        kv_far(i).start()
        kv_sib(i).start()

    start_kv(0)
    q_copy.start()
    each(HEADS, lambda i: kv_own(i).start())

    def base_of(s):
        g = span[0, s]
        return s - jnp.where(g == 1, 0, jnp.where(g == 2, s % 2, s % 4))

    my_base = base_of(me)
    place = lax.broadcasted_iota(jnp.int32, (8, TOK), 1)
    for r, s in enumerate((me, sib, far, cross)):
        base = base_of(s)
        live = jnp.where(base == my_base, clip[0, s] - (s - base) * TOK, 0)
        bias_s[:, r * TOK : (r + 1) * TOK] = jnp.where(place < live, 0.0, FLOOR)

    pair_wait.wait_recv()
    w_tmp[...] = jnp.zeros_like(w_tmp)
    own_rows = w_own[:, mine].astype(F32)
    their_rows = jnp.where(c == 0, w_pair[1, 0:DEV_ROWS], w_pair[0, 0:DEV_ROWS])
    w_tmp[0:DEV_ROWS] = jnp.where(c == 0, own_rows, their_rows)
    w_tmp[DEV_ROWS:CHIP_ROWS] = jnp.where(c == 0, their_rows, own_rows)
    w_x[x] = w_tmp[...].astype(BF16)
    for d in range(1, NX):
        x_copy(d).start()
    start_kv(1)
    for d in range(1, NX):
        x_wait(d).wait_recv()
    for k in range(NX):
        w_slab[k * CHIP_ROWS : (k + 1) * CHIP_ROWS] = w_x[k].astype(F32)[0:CHIP_ROWS]
    slab(y, z)[...] = w_slab[...].astype(BF16)
    for i in range(2):
        z_copy(z_order(i)).start()
    y_copy(0, 0).start()
    y_copy(0, 1).start()

    q_copy.wait()
    each(HEADS, lambda i: kv_own(i).wait())

    def scores_of(i):
        keys = kv[i, :, :, 0:DIM].reshape(4 * TOK, DIM)
        raw = mm(q_s[head(i)], keys, NT)
        return raw * (SCALE * LOG2E) + bias_s[0:1, :]

    def o_columns(i):
        return pl.ds(pl.multiple_of(head(i) * DIM, DIM), DIM)

    def pair_sum(i):
        g_pair(i).wait_recv()
        return g_own[i] + g_recv[i].astype(F32)

    def g_stage(part):
        def opposite_head(k):
            gy_send[k] = pair_sum(k).astype(BF16)
            g_half(k, 0).start()
            g_half(k, 1).start()

        def next_head(way, k):
            i = OWN_HEADS * (1 + way) + k
            total = pair_sum(i)
            g_half(k, way).wait_recv()
            here = slice(way * QUARTER, (way + 1) * QUARTER)
            there = slice((1 - way) * QUARTER, (2 - way) * QUARTER)
            gy_send[i, :, there] = total[:, there].astype(BF16)
            gy_send[i, :, here] = (total[:, here] + gr_recv[way, k].astype(F32)).astype(BF16)
            g_y(k, way).start()

        def own_head(k):
            g_acc[k] = pair_sum(3 * OWN_HEADS + k)

        steps = (
            opposite_head,
            functools.partial(next_head, 0),
            functools.partial(next_head, 1),
            own_head,
        )
        each(OWN_HEADS, steps[part])

    def arrive(i):
        @pl.when(i + AHEAD < HEADS)
        def _():
            start_kv(jnp.minimum(i + AHEAD, HEADS - 1))

        kv_far(i).wait_recv()
        kv_relay(i).start()

    def forward(i):
        kv_sib(i).wait_recv()
        kv_relay(i).wait_recv()
        scores = scores_of(i)
        top = jnp.max(scores, axis=1, keepdims=True)
        weights = jnp.exp2(scores - top)
        total = jnp.sum(weights, axis=1, keepdims=True)
        lse_s[i] = top + jnp.log2(total)
        probs = (weights * (1.0 / total)).astype(BF16)
        values = kv[i, :, :, DIM:].reshape(4 * TOK, DIM)
        attended = mm(probs, values, NN).astype(BF16)
        o_s[:, o_columns(i)] = attended
        g_send[i] = mm(attended, gp[0, :, other], TN).astype(BF16)
        g_pair(i).start()
        g_own[i] = mm(attended, gp[0, :, mine], TN)

    def far_send(i):
        d_pair(i).wait_recv()
        d_x[i] = (d_rs[i % 2] + d_sib_r[i, 1].astype(F32)).astype(BF16)
        d_far(i).start()

    def backward(b):
        i = back_order(b)

        @pl.when(b >= 1)
        def _():
            far_send(jnp.maximum(b - 1, 0))

        h = head(i)
        w_head = w_all[pl.ds(pl.multiple_of(h * DIM, DIM), DIM), :]
        grad_att = mm(gp[0], w_head, NT).astype(BF16)
        delta = jnp.sum(grad_att.astype(F32) * o_s[:, o_columns(i)].astype(F32), axis=1, keepdims=True)
        probs = jnp.exp2(scores_of(i) - lse_s[i])
        values = kv[i, :, :, DIM:].reshape(4 * TOK, DIM)
        dprobs = mm(grad_att, values, NT)
        dscores = (probs * (dprobs - delta)).astype(BF16)
        probs_b = probs.astype(BF16)
        keys = kv[i, :, :, 0:DIM].reshape(4 * TOK, DIM)
        grad_o[0, h, :, 0:DIM] = (mm(dscores, keys, NN) * SCALE).astype(BF16)
        dk = mm(dscores, q_s[h], TN) * SCALE
        dv = mm(probs_b, grad_att, TN)
        d_own[b, :, 0:DIM] = dk[0:TOK]
        d_own[b, :, DIM:] = dv[0:TOK]
        d_sib[b, 0, :, 0:DIM] = dk[TOK : 2 * TOK].astype(BF16)
        d_sib[b, 0, :, DIM:] = dv[TOK : 2 * TOK].astype(BF16)
        d_sib[b, 1, :, 0:DIM] = dk[3 * TOK :].astype(BF16)
        d_sib[b, 1, :, DIM:] = dv[3 * TOK :].astype(BF16)
        d_pair(b).start()
        d_rs[b % 2, :, 0:DIM] = dk[2 * TOK : 3 * TOK]
        d_rs[b % 2, :, DIM:] = dv[2 * TOK : 3 * TOK]

    def pass_slab(n):
        d = z_order(n)
        z_wait(d).wait_recv()
        y_copy(d, 0).start()
        y_copy(d, 1).start()

    def relay_slab(d):
        y_wait(d, 0).wait_recv()
        y_wait(d, 1).wait_recv()
        y_relay(d).start()

    def weight_step(t):
        for n in WEIGHT_SEND.get(t, ()):
            z_copy(z_order(n)).start()
        for n in WEIGHT_PASS.get(t, ()):
            pass_slab(n)
        for n in WEIGHT_RELAY.get(t, ()):
            relay_slab(0 if n == 0 else z_order(n - 1))
        if t == WEIGHT_OWN:
            block_copy(0).start()
        if t == WEIGHT_NEAR:
            block_copy(1).start()
            block_copy(2).start()
        if t == WEIGHT_LAST:
            for d in range(NZ):
                y_relay_wait(d).wait_recv()
            block_copy(3).start()

    def own_sum():
        g_stage(3)
        for k in range(OWN_HEADS):
            g_y(k, 0).wait_recv()
            g_y(k, 1).wait_recv()
            total = g_acc[k] + gy_recv[0, k].astype(F32) + gy_recv[1, k].astype(F32)
            g_acc[k] = total
            gz_send[k * DIM : (k + 1) * DIM] = total.astype(BF16)

    def step(t):
        @pl.when(t < HEADS)
        def _():
            i = jnp.minimum(t, HEADS - 1)
            arrive(i)

        for at in range(WEIGHT_LAST + 1):

            @pl.when(t == at)
            def _(at=at):
                weight_step(at)

        for part, at in enumerate(G_AT):

            @pl.when(t == at)
            def _(part=part):
                g_stage(part)

        @pl.when(t == GZ_AT)
        def _():
            own_sum()

        for part in range(4):

            @pl.when(t == GZ_AT + part)
            def _(part=part):
                for n in (2 * part, 2 * part + 1)[: NZ - 1 - 2 * part]:
                    g_z(z_order(n)).start()

        for k in range(4):

            @pl.when(t == LAG + OWN_HEADS * k)
            def _(k=k):
                block_wait(k).wait_recv()

        @pl.when(t < HEADS)
        def _():
            forward(jnp.minimum(t, HEADS - 1))

        @pl.when(t >= LAG)
        def _():
            backward(jnp.maximum(t - LAG, 0))

    each(HEADS + LAG, step)
    far_send(HEADS - 1)

    def project(k):
        columns = pl.ds(pl.multiple_of(k * TOK, TOK), TOK)
        proj_o[0, :, columns] = mm(o_s[...], w_all[:, columns], NN).astype(BF16)

    each(WIDTH // TOK, project)

    def finish(i):
        d_far(i).wait_recv()
        total = d_own[i] + d_sib_r[i, 0].astype(F32) + d_x_r[i].astype(F32)
        grad_o[0, head(back_order(i)), :, DIM:] = total.astype(BF16)

    each(3, finish)

    for d in range(1, NZ):
        g_z(d).wait_recv()
    acc = g_acc.reshape(BLOCK, HALF)
    total = acc[pl.ds(pl.multiple_of(SLAB * z, 8), SLAB)]
    for d in range(1, NZ):
        total = total + gz_recv[d - 1].astype(F32)
    gx_in[...] = total
    for k in range(NX):
        gx_send[k] = jnp.zeros_like(gx_send[k])
        gx_send[k, 0:CHIP_ROWS] = gx_in[k * CHIP_ROWS : (k + 1) * CHIP_ROWS]
    for d in range(1, NX):
        g_x(d).start()

    each(3, lambda i: finish(i + 3))

    for d in range(1, NX):
        g_x(d).wait_recv()
    total = gx_send[x]
    for d in range(1, NX):
        total = total + gx_recv[d - 1]
    for k in range(2):
        gc_send[k] = jnp.zeros_like(gc_send[k])
        gc_send[k, 0:DEV_ROWS] = total[k * DEV_ROWS : (k + 1) * DEV_ROWS]
    g_c.start()

    each(HEADS - 6, lambda i: finish(i + 6))

    g_c.wait_recv()
    gw_o[:, mine] = gc_send[c, 0:DEV_ROWS]
    gw_o[:, other] = gc_recv[0:DEV_ROWS]

    def sent(i):
        kv_far(i).wait_send()
        kv_sib(i).wait_send()
        kv_relay(i).wait_send()
        g_pair(i).wait_send()
        d_pair(i).wait_send()
        d_far(i).wait_send()

    each(HEADS, sent)

    def sent_g(k):
        for way in range(2):
            g_half(k, way).wait_send()
            g_y(k, way).wait_send()

    each(OWN_HEADS, sent_g)
    pair_copy.wait_send()
    g_c.wait_send()
    for d in range(1, NX):
        x_copy(d).wait_send()
        g_x(d).wait_send()
    for d in range(1, NZ):
        z_copy(d).wait_send()
        g_z(d).wait_send()

    def sent_y(d):
        y_copy(d, 0).wait_send()
        y_copy(d, 1).wait_send()
        y_relay(d).wait_send()

    each(NZ, sent_y)
    for k in range(4):
        block_copy(k).wait_send()


def hand_over(proj, grad, gw, proj_o, grad_o, gw_o, sems):
    copies = [pltpu.make_async_copy(gw, gw_o, sems.at[0])]
    for k in range(2):
        rows = pl.ds(k * (TOK // 2), TOK // 2)
        copies.append(pltpu.make_async_copy(proj.at[0, rows], proj_o.at[0, rows], sems.at[1 + k]))
    for h in range(HEADS):
        copies.append(pltpu.make_async_copy(grad.at[0, h], grad_o.at[0, h], sems.at[3 + h]))
    for copy in copies:
        copy.start()
    for copy in copies:
        copy.wait()


def local(qkv, out_weight, grad_projected, group_span, clip_length):
    vmem = functools.partial(pl.BlockSpec, memory_space=pltpu.VMEM)
    smem = functools.partial(pl.BlockSpec, memory_space=pltpu.SMEM)
    sem = pltpu.SemaphoreType.DMA
    scratch = [
        pltpu.VMEM((HEADS, TOK, DIM), BF16),
        pltpu.VMEM((HEADS, 4, TOK, 2 * DIM), BF16),
        pltpu.VMEM((8, 4 * TOK), F32),
        pltpu.VMEM((WIDTH, WIDTH), BF16),
        pltpu.VMEM((TOK, WIDTH), BF16),
        pltpu.VMEM((HEADS, TOK, 1), F32),
        pltpu.VMEM((8, HALF), F32),
        pltpu.VMEM((2, 8, HALF), F32),
        pltpu.VMEM((16, HALF), F32),
        pltpu.VMEM((NX, 16, HALF), BF16),
        pltpu.VMEM((SLAB, HALF), F32),
        pltpu.VMEM((HEADS, DIM, HALF), F32),
        pltpu.VMEM((OWN_HEADS, DIM, HALF), F32),
        pltpu.VMEM((HEADS, DIM, HALF), BF16),
        pltpu.VMEM((HEADS, DIM, HALF), BF16),
        pltpu.VMEM((HEADS - OWN_HEADS, DIM, HALF), BF16),
        pltpu.VMEM((2, OWN_HEADS, DIM, QUARTER), BF16),
        pltpu.VMEM((2, OWN_HEADS, DIM, HALF), BF16),
        pltpu.VMEM((BLOCK, HALF), BF16),
        pltpu.VMEM((NZ - 1, SLAB, HALF), BF16),
        pltpu.VMEM((SLAB, HALF), F32),
        pltpu.VMEM((NX, 16, HALF), F32),
        pltpu.VMEM((NX - 1, 16, HALF), F32),
        pltpu.VMEM((2, 8, HALF), F32),
        pltpu.VMEM((8, HALF), F32),
        pltpu.VMEM((HEADS, TOK, 2 * DIM), F32),
        pltpu.VMEM((2, TOK, 2 * DIM), F32),
        pltpu.VMEM((HEADS, 2, TOK, 2 * DIM), BF16),
        pltpu.VMEM((HEADS, 2, TOK, 2 * DIM), BF16),
        pltpu.VMEM((HEADS, TOK, 2 * DIM), BF16),
        pltpu.VMEM((HEADS, TOK, 2 * DIM), BF16),
        sem((1 + HEADS,)),
        sem((HEADS,)), sem((HEADS,)),
        sem((HEADS,)), sem((HEADS,)),
        sem((HEADS,)), sem((HEADS,)),
        sem, sem,
        sem((NX - 1,)), sem((NX - 1,)),
        sem((NZ - 1,)), sem((NZ - 1,)),
        sem((NZ, 2)), sem((NZ, 2)),
        sem((NZ,)), sem((NZ,)),
        sem((4,)), sem((4,)),
        sem((HEADS,)), sem((HEADS,)),
        sem((OWN_HEADS, 2)), sem((OWN_HEADS, 2)),
        sem((OWN_HEADS, 2)), sem((OWN_HEADS, 2)),
        sem((NZ - 1,)), sem((NZ - 1,)),
        sem((NX - 1,)), sem((NX - 1,)),
        sem, sem,
        sem((HEADS,)), sem((HEADS,)),
        sem((HEADS,)), sem((HEADS,)),
    ]
    results = pl.pallas_call(
        kernel,
        out_shape=(
            jax.ShapeDtypeStruct((1, TOK, WIDTH), BF16),
            jax.ShapeDtypeStruct((1, HEADS, TOK, 3 * DIM), BF16),
            jax.ShapeDtypeStruct((DEV_ROWS, WIDTH), F32),
        ),
        in_specs=[pl.BlockSpec(memory_space=pl.ANY), vmem(), vmem(), smem(), smem()],
        out_specs=(vmem(), vmem(), vmem()),
        scratch_shapes=scratch,
        compiler_params=pltpu.CompilerParams(
            collective_id=0, has_side_effects=True, vmem_limit_bytes=60 * 1024 * 1024
        ),
        cost_estimate=pl.CostEstimate(flops=10**10, bytes_accessed=10**7, transcendentals=7 * 10**6),
    )(qkv, out_weight, grad_projected, group_span, clip_length)
    hbm = functools.partial(pl.BlockSpec, memory_space=pl.ANY)
    return pl.pallas_call(
        hand_over,
        out_shape=tuple(jax.ShapeDtypeStruct(r.shape, r.dtype) for r in results),
        in_specs=[vmem(), vmem(), vmem()],
        out_specs=(hbm(), hbm(), hbm()),
        scratch_shapes=[sem((HEADS + 3,))],
    )(*results)


def solution(mesh):
    in_specs = (
        P("dp", None, "seq", None),
        P(("dp", "seq"), None),
        P("dp", "seq", None),
        P("dp", None),
        P("dp", None),
    )
    out_specs = (P("dp", "seq", None), P("dp", None, "seq", None), P(("dp", "seq"), None))
    return jax.shard_map(local, mesh=mesh, in_specs=in_specs, out_specs=out_specs, check_vma=False)
```
